512 devices in a mesh: fiber: 512 (over y, x, z, core).
Axes of the slice: x: 4, y: 8, z: 8, core: 2. Of those that a mesh axis runs over, the one named last changes fastest.
Arguments:
- traces: float32 [16384, 3000], P('fiber'), may hold values from -16 to 16
- live: int32 [16384], P('fiber'), may hold values 0 or 1
- segment: int32 [16384], P('fiber'), may hold values from 0 to 340, never falling along the last dimension, each value on 1 to 96 neighbouring positions
Outputs:
- correlations: bfloat16 [16384, 128, 256], P('fiber')
The draws below stay inside these ranges and needn't reach their ends.
Inputs may be any that keep to these rules, and one draw needn't show every extreme that they name: `live`: 1 marks a working channel. segment numbers never fall along the fiber, and a segment holds 1 to 96 channels.
All inputs are finite; a program needn't handle non-finite values. No bound on the sum of `live` on one device may be relied on, other than what follows from the above.
Results may differ from the reference program's by a relative error of at most 0.0071.
Values may be sent and summed in bfloat16 or wider, within the bound.
A program may use at most 64 MiB of HBM per device.

```python
import math
import jax
import jax.numpy as jnp
import numpy as np
from jax import lax

CH_DEV = 32
NT = 3000
LOW_BIN = 32
FB = 768
BAND = 64
HALF_WIN = 15
LAGS = 256
PARTNERS = 128
NCH = 16384
N_FIBER = 512


def draw_traces(key, part):
    key = jax.random.fold_in(key, 11)
    scale_key, sample_key = jax.random.split(key)
    scales = jnp.exp(jax.random.uniform(scale_key, (NCH, 1), jnp.float32, math.log(0.25), math.log(4.0)))
    samples = jnp.clip(jax.random.normal(sample_key, (NCH, NT), jnp.float32), -4.0, 4.0)
    return samples * scales


def place_ends(entries, stream_key, smallest, top_value):
    dims = entries.shape
    place = [jax.random.randint(jax.random.fold_in(stream_key, axis), (), 0, dims[axis]) for axis in range(len(dims))]
    entries = entries.at[tuple(place)].set(smallest)
    longest = dims.index(max(dims))
    place[longest] = (place[longest] + 1) % dims[longest]
    return entries.at[tuple(place)].set(top_value)


def split_up(amount, total, most, lean):
    portions = [(1 << 20) // math.isqrt(standing ** lean) + 1 for standing in range(2, amount + 1)]
    spare, given = total - most - (amount - 1), [1] * (amount - 1)
    while spare > 0:
        movable = [i for i in range(amount - 1) if given[i] < most]
        mass, left = sum([portions[i] for i in movable]), spare
        for i in movable:
            extra = min(most - given[i], max(1, left * portions[i] // mass), spare)
            given[i] = given[i] + extra
            spare = spare - extra
    return np.array([most] + given)


def ragged_sizes(own_key, number_of, total, limit, lean):
    if number_of == 2:
        one = jax.random.randint(own_key, (), max(1, total - limit), min(limit, total - 1) + 1)
        return jnp.stack([one, total - one])
    tallies = jnp.asarray(split_up(number_of, total, limit, lean), jnp.int32)
    twos = (number_of - 1) // 2
    giver, sink = tallies[1:1 + 2 * twos:2], tallies[2:2 + 2 * twos:2]
    slack = jnp.minimum(giver - 1, limit - sink)
    passed = jax.random.randint(jax.random.fold_in(own_key, 1), (twos,), 0, 1 << 20) % (slack + 1)
    tallies = tallies.at[1:1 + 2 * twos:2].set(giver - passed).at[2:2 + 2 * twos:2].set(sink + passed)
    return tallies[jax.random.permutation(jax.random.fold_in(own_key, 2), number_of)]


def setup_inputs(seed: int = 0) -> dict:
    seeds = jax.random.split(jax.random.key(seed), 4)
    traces = draw_traces(jax.random.fold_in(seeds[3], 71), 0)
    live = place_ends((jax.random.randint(seeds[1], (NCH,), 0, 16) < 15).astype(jnp.int32), jax.random.fold_in(seeds[1], 1), 0, 1)
    segment = jnp.searchsorted(jnp.cumsum(ragged_sizes(seeds[2], NCH // 48, NCH, 96, 2)), jnp.arange(NCH), side="right").astype(jnp.int32)
    return {"traces": traces, "live": live, "segment": segment}


def lag_weights(length_total):
    bin_index = LOW_BIN + jnp.arange(FB, dtype=jnp.int32)
    lag_index = jnp.arange(LAGS, dtype=jnp.int32) - LAGS // 2
    phases = jnp.mod(bin_index[:, None] * lag_index[None, :], length_total).astype(jnp.float32) * (2.0 * math.pi / length_total)
    scaled = jnp.concatenate([jnp.cos(phases), -jnp.sin(phases)], axis=0) / math.sqrt(FB)
    return scaled.astype(jnp.bfloat16)

def cross_spectra(own_rows, partner_rows):
    own_real = own_rows[:, None, :FB].astype(jnp.float32)
    own_imag = own_rows[:, None, FB:].astype(jnp.float32)
    partner_real = partner_rows[None, :, :FB].astype(jnp.float32)
    partner_imag = partner_rows[None, :, FB:].astype(jnp.float32)
    real_cross = (own_real * partner_real + own_imag * partner_imag).astype(jnp.bfloat16)
    imag_cross = (own_imag * partner_real - own_real * partner_imag).astype(jnp.bfloat16)
    return jnp.concatenate([real_cross, imag_cross], axis=2)

def reference(traces, live, segment):
    channels = traces.shape[0]
    live_float = live.astype(jnp.float32)[:, None]
    values = traces * live_float
    padded_values = jnp.pad(values, ((HALF_WIN, HALF_WIN), (0, 0)))
    padded_live = jnp.pad(live, HALF_WIN)
    padded_segment = jnp.pad(segment, HALF_WIN, constant_values=-1)
    totals = jnp.zeros_like(values)
    counted = jnp.zeros((channels,), jnp.int32)
    for offset in range(2 * HALF_WIN + 1):
        keep = (padded_live[offset:offset + channels] == 1) & (padded_segment[offset:offset + channels] == segment)
        totals = totals + jnp.where(keep[:, None], padded_values[offset:offset + channels], 0.0)
        counted = counted + keep.astype(jnp.int32)
    local_mean = totals / jnp.maximum(counted, 1).astype(jnp.float32)[:, None]
    filtered = live_float * (values - local_mean)
    taper = jnp.sin(math.pi * (jnp.arange(FB, dtype=jnp.float32) + 0.5) / FB)
    full = jnp.fft.rfft(filtered, axis=1)[:, LOW_BIN:LOW_BIN + FB]
    real_part = jnp.real(full).astype(jnp.float32) * taper
    imag_part = jnp.imag(full).astype(jnp.float32) * taper
    power = (real_part * real_part + imag_part * imag_part).reshape(channels, FB // BAND, BAND).mean(axis=2)
    amplitude = jnp.repeat(jnp.sqrt(power + 1.0), BAND, axis=1)
    whitened = jnp.concatenate([real_part / amplitude, imag_part / amplitude], axis=1).astype(jnp.bfloat16)
    padded = jnp.concatenate([whitened, jnp.zeros((PARTNERS, 2 * FB), jnp.bfloat16)], axis=0)
    table = lag_weights(NT)

    def one_block(block):
        start = (block * CH_DEV).astype(jnp.int32)
        own_rows = lax.dynamic_slice_in_dim(whitened, start, CH_DEV, 0)
        partner_rows = lax.dynamic_slice_in_dim(padded, (start + CH_DEV).astype(jnp.int32), PARTNERS, 0)
        cross = cross_spectra(own_rows, partner_rows).reshape(CH_DEV * PARTNERS, 2 * FB)
        result = jnp.dot(cross, table, preferred_element_type=jnp.float32)
        return result.astype(jnp.bfloat16).reshape(CH_DEV, PARTNERS, LAGS)
    blocks = lax.map(one_block, jnp.arange(N_FIBER, dtype=jnp.int32))
    return blocks.reshape(NCH, PARTNERS, LAGS)
```

```python
import functools
import math

import jax
import jax.numpy as jnp
import ml_dtypes
import numpy as np
from jax import lax
from jax.experimental import pallas as pl
from jax.experimental.pallas import tpu as pltpu
from jax.sharding import PartitionSpec as P

LOW_BIN = 32
FB = 768
BAND = 64
HALF_WIN = 15
LAGS = 256
CH = 32
HALF = 16
REACH = 4
SPAN = 256
CHUNK = 256
WHITEN_EPS = 1.0
MESH = pl.DeviceIdType.MESH


def tables(length):
    bins = LOW_BIN + np.arange(FB)
    taper = np.sin(np.pi * (np.arange(FB) + 0.5) / FB)
    angle = 2.0 * np.pi / length * np.mod(np.arange(SPAN)[:, None] * bins[None, :], length)
    base = np.concatenate([np.cos(angle) * taper, -np.sin(angle) * taper], axis=1)
    high = base.astype(ml_dtypes.bfloat16)
    low = (base - high.astype(np.float64)).astype(ml_dtypes.bfloat16)
    turn = 2.0 * np.pi / length * np.mod(SPAN * bins, length)
    twiddle = np.stack([np.cos(turn), -np.sin(turn)]).astype(np.float32)
    band = np.arange(CHUNK) // BAND
    same = (band[:, None] == band[None, :]).astype(ml_dtypes.bfloat16)
    lag = np.arange(LAGS) - LAGS // 2
    phase = 2.0 * np.pi / length * np.mod(bins[:, None] * lag[None, :], length)
    lags = np.concatenate([np.cos(phase), -np.sin(phase)], axis=0) / math.sqrt(FB)
    return high, low, twiddle, same, lags.astype(np.float32).astype(ml_dtypes.bfloat16)


def split3(value):
    first = value.astype(jnp.bfloat16)
    rest = value - first.astype(jnp.float32)
    second = rest.astype(jnp.bfloat16)
    third = (rest - second.astype(jnp.float32)).astype(jnp.bfloat16)
    return first, second, third


def dot(a, b):
    return jnp.dot(a, b, preferred_element_type=jnp.float32)


def spectra_kernel(
    count,
    traces_hbm, live_ref, segment_ref, high_hbm, low_hbm, twiddle_ref, same_ref,
    rows_ref,
    traces, high, low, first, second, spec, labels, whole,
    in_sem, here_sem, halo_send, halo_recv, row_send, row_recv,
):
    me = lax.axis_index("fiber")
    core = lax.rem(me, 2)
    depth = lax.rem(me // 2, 8)
    length = traces.shape[1]
    spans = -(-length // SPAN)

    loads = [
        pltpu.make_async_copy(traces_hbm, traces, in_sem.at[0]),
        pltpu.make_async_copy(high_hbm, high, in_sem.at[1]),
        pltpu.make_async_copy(low_hbm, low, in_sem.at[2]),
    ]
    for load in loads:
        load.start()

    barrier = pltpu.get_barrier_semaphore()

    def exists(step):
        return (me + step >= 0) & (me + step < count)

    def on(condition, action):
        pl.when(condition)(action)

    for step in (1, 2, 4):
        on(
            exists(-step),
            lambda: pl.semaphore_signal(barrier, inc=1, device_id=(me - step,), device_id_type=MESH),
        )

    def greet():
        peers = sum(jnp.where(exists(step), 1, 0) for step in (1, 2, 4))
        on(exists(1), lambda: pl.semaphore_wait(barrier, peers))
        for slot, step in enumerate((1, 2, 4)):
            on(
                exists(step),
                lambda: pl.semaphore_signal(
                    here_sem.at[slot], inc=1, device_id=(me + step,), device_id_type=MESH
                ),
            )

    whole[...] = jnp.zeros_like(whole)
    whole[0:1, 0:CH] = segment_ref[...] * 2 + live_ref[...]
    packed = whole[...]
    lane = lax.broadcasted_iota(jnp.int32, (8, 128), 1)
    own_labels = pltpu.roll(packed, HALF, 1)
    labels[0] = own_labels
    labels[1] = jnp.where(lane < HALF, pltpu.roll(packed, 128 - HALF, 1), 0)
    labels[2] = jnp.where((lane >= CH + HALF) & (lane < CH + 2 * HALF), pltpu.roll(packed, CH + HALF, 1), 0)

    last = depth == 7
    on(last, greet)

    loads[0].wait()
    for s in range(spans):
        piece = traces[:, s * SPAN : min(length, (s + 1) * SPAN)]
        if piece.shape[1] < SPAN:
            piece = jnp.concatenate([piece, jnp.zeros((CH, SPAN - piece.shape[1]), jnp.float32)], axis=1)
        top = piece.astype(jnp.bfloat16)
        first[s * CH : (s + 1) * CH, :] = top
        second[s * CH : (s + 1) * CH, :] = (piece - top.astype(jnp.float32)).astype(jnp.bfloat16)
    loads[1].wait()
    loads[2].wait()
    for c in range(FB // CHUNK):
        parts = []
        for offset in (c * CHUNK, FB + c * CHUNK):
            cols = slice(offset, offset + CHUNK)
            parts.append(
                dot(first[...], high[:, cols]) + dot(second[...], high[:, cols]) + dot(first[...], low[:, cols])
            )
        cosine = twiddle_ref[0:1, c * CHUNK : (c + 1) * CHUNK]
        sine = twiddle_ref[1:2, c * CHUNK : (c + 1) * CHUNK]
        real = parts[0][(spans - 1) * CH :, :]
        imag = parts[1][(spans - 1) * CH :, :]
        for s in range(spans - 2, -1, -1):
            rows = slice(s * CH, (s + 1) * CH)
            real, imag = (
                parts[0][rows, :] + (real * cosine - imag * sine),
                parts[1][rows, :] + (real * sine + imag * cosine),
            )
        spec[HALF : HALF + CH, c * CHUNK : (c + 1) * CHUNK] = real
        spec[HALF : HALF + CH, FB + c * CHUNK : FB + (c + 1) * CHUNK] = imag

    on(jnp.logical_not(last), greet)

    def remote(src, dst, send, recv, target):
        return pltpu.make_async_remote_copy(
            src_ref=src, dst_ref=dst, send_sem=send, recv_sem=recv, device_id=(target,), device_id_type=MESH
        )

    right = [
        remote(spec.at[pl.ds(CH, HALF)], spec.at[pl.ds(0, HALF)], halo_send.at[0], halo_recv.at[0], me + 1),
        remote(labels.at[1], labels.at[3], halo_send.at[1], halo_recv.at[1], me + 1),
    ]
    left = [
        remote(spec.at[pl.ds(HALF, HALF)], spec.at[pl.ds(CH + HALF, HALF)], halo_send.at[2], halo_recv.at[2], me - 1),
        remote(labels.at[2], labels.at[4], halo_send.at[3], halo_recv.at[3], me - 1),
    ]

    def start_all(copies):
        for copy in copies:
            copy.start()

    on(exists(1), lambda: start_all(right))

    def send_left():
        pl.semaphore_wait(here_sem.at[0], 1)
        start_all(left)

    late = (depth == 0) & (core == 0)
    on(exists(-1) & jnp.logical_not(late), send_left)

    def row_slice(block, half):
        return rows_ref.at[pl.ds(block * CH + half * HALF, HALF)]

    def row_copy(kind, half, source, target_block, target):
        return remote(
            row_slice(source, half), row_slice(target_block, half),
            row_send.at[kind, half], row_recv.at[target_block - 1, half], target,
        )

    def own_copies(half):
        return [
            (row_copy(0, half, 0, 1, me - 1), core == 1),
            (row_copy(1, half, 0, 2, me - 2), exists(-2)),
            (row_copy(2, half, 0, 4, me - 4), exists(-4)),
        ]

    wide_row = lax.broadcasted_iota(jnp.int32, (CH, 128), 0) + HALF
    wide_lane = lax.broadcasted_iota(jnp.int32, (CH, 128), 1)
    near = jnp.abs(wide_lane - wide_row) <= HALF_WIN

    def whiten(half, received):
        base = half * HALF
        mine = jnp.where(wide_lane == wide_row, labels[0, 0:1, :], 0).astype(jnp.float32)
        mine = jnp.sum(mine, axis=1, keepdims=True).astype(jnp.int32)
        wide = labels[0, 0:1, :] + received
        keep = near & ((wide >> 1) == (mine >> 1)) & ((wide & 1) == 1)
        inside = jnp.where(keep, 1.0, 0.0)
        divisor = jnp.maximum(jnp.sum(inside, axis=1, keepdims=True), 1.0)[base : base + HALF]
        alive = (mine & 1).astype(jnp.float32)[base : base + HALF]
        weights = inside[base : base + HALF, base : base + 3 * HALF].astype(jnp.bfloat16)
        weights = jnp.concatenate([weights, weights, weights], axis=1)
        for c in range(FB // CHUNK):
            parts = []
            for offset in (c * CHUNK, FB + c * CHUNK):
                cols = slice(offset, offset + CHUNK)
                stack = jnp.concatenate(split3(spec[base : base + 3 * HALF, cols]), axis=0)
                total = dot(weights, stack)
                value = spec[HALF + base : 2 * HALF + base, cols]
                parts.append(alive * (value * alive - total / divisor))
            square = parts[0] * parts[0] + parts[1] * parts[1]
            sums = dot(jnp.concatenate(split3(square), axis=0), same_ref[...])
            power = (sums[:HALF] + (sums[HALF : 2 * HALF] + sums[2 * HALF :])) * (1.0 / BAND)
            scale = lax.rsqrt(power + WHITEN_EPS)
            rows_ref[base : base + HALF, c * CHUNK : (c + 1) * CHUNK] = (parts[0] * scale).astype(jnp.bfloat16)
            rows_ref[base : base + HALF, FB + c * CHUNK : FB + (c + 1) * CHUNK] = (parts[1] * scale).astype(jnp.bfloat16)

    def receive(copies):
        for copy in copies:
            copy.wait_recv()

    def blank(ref_rows):
        rows_ref[ref_rows, :] = jnp.zeros((CH, 2 * FB), jnp.bfloat16)

    for block in range(1, REACH + 1):
        on(jnp.logical_not(exists(block)), functools.partial(blank, slice(block * CH, (block + 1) * CH)))

    def no_right():
        spec[CH + HALF :, :] = jnp.zeros((HALF, 2 * FB), jnp.float32)
        labels[4] = jnp.zeros((8, 128), jnp.int32)

    def no_left():
        spec[0:HALF, :] = jnp.zeros((HALF, 2 * FB), jnp.float32)
        labels[3] = jnp.zeros((8, 128), jnp.int32)

    on(exists(1), lambda: receive(left))
    on(jnp.logical_not(exists(1)), no_right)
    whiten(1, labels[4, 0:1, :])
    on(exists(-1) & late, send_left)
    on(core == 1, own_copies(1)[0][0].start)

    def meet(slot):
        pl.semaphore_wait(here_sem.at[slot], 1)

    on(exists(-2), lambda: meet(1))
    on(exists(-2), own_copies(1)[1][0].start)
    on(exists(-4), lambda: meet(2))
    on(exists(-4), own_copies(1)[2][0].start)

    on(exists(-1), lambda: receive(right))
    on(jnp.logical_not(exists(-1)), no_left)
    whiten(0, labels[3, 0:1, :])
    for copy, condition in own_copies(0):
        on(condition, copy.start)

    def arrived(block, half):
        row_copy(0, half, 0, block, me).wait_recv()

    passed = []
    for half in (1, 0):
        on(exists(2), functools.partial(arrived, 2, half))
        to_high = row_copy(3, half, 2, 1, me + 1)
        to_low = row_copy(3, half, 2, 3, me - 1)
        on(exists(2) & (core == 0), to_high.start)
        on(exists(2) & (core == 1), to_low.start)
        passed += [(to_high, exists(2))]
    for half in (1, 0):
        on(exists(4), functools.partial(arrived, 4, half))
        to_high = row_copy(4, half, 4, 3, me + 1)
        on(exists(4) & (core == 0), to_high.start)
        passed += [(to_high, exists(4) & (core == 0))]
    for block in (1, 3):
        for half in (1, 0):
            on(exists(block), functools.partial(arrived, block, half))

    def sent(copies):
        for copy in copies:
            copy.wait_send()

    on(exists(1), lambda: sent(right))
    on(exists(-1), lambda: sent(left))
    for half in (1, 0):
        for copy, condition in own_copies(half):
            on(condition, copy.wait_send)
    for copy, condition in passed:
        on(condition, copy.wait_send)


GROUP = 8


def correlate_kernel(rows_ref, table_ref, out_ref):
    group = pl.program_id(0)
    own = rows_ref[pl.ds(pl.multiple_of(lax.div(group, 2) * HALF, HALF), HALF), :].astype(jnp.float32)
    own = jnp.where(lax.rem(group, 2) == 0, own[:GROUP], own[GROUP:])
    total = None
    for c in range(FB // CHUNK):
        re_cols = slice(c * CHUNK, (c + 1) * CHUNK)
        im_cols = slice(FB + c * CHUNK, FB + (c + 1) * CHUNK)
        own_re = own[:, None, re_cols]
        own_im = own[:, None, im_cols]
        far_re = rows_ref[CH:, re_cols].astype(jnp.float32)[None]
        far_im = rows_ref[CH:, im_cols].astype(jnp.float32)[None]
        real = (own_re * far_re + own_im * far_im).astype(jnp.bfloat16).reshape(GROUP * REACH * CH, CHUNK)
        imag = (own_im * far_re - own_re * far_im).astype(jnp.bfloat16).reshape(GROUP * REACH * CH, CHUNK)
        term = dot(real, table_ref[re_cols, :]) + dot(imag, table_ref[im_cols, :])
        total = term if total is None else total + term
    out_ref[...] = total.astype(jnp.bfloat16).reshape(GROUP, REACH * CH, LAGS)


def on_device(traces, live, segment):
    count = lax.axis_size("fiber")
    channels, length = traces.shape
    high, low, twiddle, same, lags = (jnp.asarray(t) for t in tables(length))
    anywhere = pl.BlockSpec(memory_space=pl.ANY)
    in_vmem = pl.BlockSpec(memory_space=pltpu.VMEM)
    spans = -(-length // SPAN)
    rows = pl.pallas_call(
        functools.partial(spectra_kernel, count),
        out_shape=jax.ShapeDtypeStruct(((1 + REACH) * channels, 2 * FB), jnp.bfloat16),
        in_specs=[anywhere, in_vmem, in_vmem, anywhere, anywhere, in_vmem, in_vmem],
        out_specs=in_vmem,
        scratch_shapes=[
            pltpu.VMEM((channels, length), jnp.float32),
            pltpu.VMEM((SPAN, 2 * FB), jnp.bfloat16),
            pltpu.VMEM((SPAN, 2 * FB), jnp.bfloat16),
            pltpu.VMEM((spans * CH, SPAN), jnp.bfloat16),
            pltpu.VMEM((spans * CH, SPAN), jnp.bfloat16),
            pltpu.VMEM((2 * CH, 2 * FB), jnp.float32),
            pltpu.VMEM((5, 8, 128), jnp.int32),
            pltpu.VMEM((8, 128), jnp.int32),
            pltpu.SemaphoreType.DMA((3,)),
            pltpu.SemaphoreType.REGULAR((3,)),
            pltpu.SemaphoreType.DMA((4,)),
            pltpu.SemaphoreType.DMA((4,)),
            pltpu.SemaphoreType.DMA((5, 2)),
            pltpu.SemaphoreType.DMA((4, 2)),
        ],
        compiler_params=pltpu.CompilerParams(
            collective_id=0, has_side_effects=True, vmem_limit_bytes=40 * 1024 * 1024
        ),
        name="spectra",
    )(traces, live.reshape(1, channels), segment.reshape(1, channels), high, low, twiddle, same)
    return pl.pallas_call(
        correlate_kernel,
        grid=(channels // GROUP,),
        out_shape=jax.ShapeDtypeStruct((channels, REACH * channels, LAGS), jnp.bfloat16),
        in_specs=[
            pl.BlockSpec(((1 + REACH) * channels, 2 * FB), lambda g: (0, 0)),
            pl.BlockSpec((2 * FB, LAGS), lambda g: (0, 0)),
        ],
        out_specs=pl.BlockSpec((GROUP, REACH * channels, LAGS), lambda g: (g, 0, 0)),
        compiler_params=pltpu.CompilerParams(vmem_limit_bytes=48 * 1024 * 1024),
        name="correlate",
    )(rows, lags)


def solution(mesh):
    return jax.shard_map(
        on_device,
        mesh=mesh,
        in_specs=(P("fiber", None), P("fiber"), P("fiber")),
        out_specs=P("fiber", None, None),
        check_vma=False,
    )
```

```python
import functools
import math

import jax
import jax.numpy as jnp
import ml_dtypes
import numpy as np
from jax import lax
from jax.experimental import pallas as pl
from jax.experimental.pallas import tpu as pltpu
from jax.sharding import PartitionSpec as P

LOW_BIN = 32
FB = 768
BAND = 64
HALF_WIN = 15
LAGS = 256
CH = 32
HALF = 16
REACH = 4
SPAN = 256
CHUNK = 256
WHITEN_EPS = 1.0
MESH = pl.DeviceIdType.MESH


CHUNKS = FB // CHUNK
WIDE = 2 * CHUNK


def chunk_major(table, axis):
    halves = np.split(table, 2, axis=axis)
    pieces = [np.split(half, CHUNKS, axis=axis) for half in halves]
    return [np.concatenate([pieces[0][c], pieces[1][c]], axis=axis) for c in range(CHUNKS)]


def tables(length):
    bins = LOW_BIN + np.arange(FB)
    taper = np.sin(np.pi * (np.arange(FB) + 0.5) / FB)
    angle = 2.0 * np.pi / length * np.mod(np.arange(SPAN)[:, None] * bins[None, :], length)
    base = np.concatenate([np.cos(angle) * taper, -np.sin(angle) * taper], axis=1)
    base = np.stack(chunk_major(base, 1))
    high = base.astype(ml_dtypes.bfloat16)
    low = (base - high.astype(np.float64)).astype(ml_dtypes.bfloat16)
    turn = 2.0 * np.pi / length * np.mod(SPAN * bins, length)
    twiddle = np.stack([np.cos(turn), -np.sin(turn)]).astype(np.float32)
    lag = np.arange(LAGS) - LAGS // 2
    phase = 2.0 * np.pi / length * np.mod(bins[:, None] * lag[None, :], length)
    lags = np.concatenate([np.cos(phase), -np.sin(phase)], axis=0) / math.sqrt(FB)
    lags = np.concatenate(chunk_major(lags.astype(np.float32), 0), axis=0)
    return np.stack([high, low], axis=1), twiddle, lags.astype(ml_dtypes.bfloat16)


def split3(value):
    first = value.astype(jnp.bfloat16)
    rest = value - first.astype(jnp.float32)
    second = rest.astype(jnp.bfloat16)
    third = (rest - second.astype(jnp.float32)).astype(jnp.bfloat16)
    return first, second, third


def dot(a, b):
    return jnp.dot(a, b, preferred_element_type=jnp.float32)


def correlate(own, far, table_ref):
    total = None
    for c in range(CHUNKS):
        re_cols = slice(c * WIDE, c * WIDE + CHUNK)
        im_cols = slice(c * WIDE + CHUNK, (c + 1) * WIDE)
        own_re = own[:, None, re_cols]
        own_im = own[:, None, im_cols]
        far_re = far(re_cols).astype(jnp.float32)[None]
        far_im = far(im_cols).astype(jnp.float32)[None]
        shape = (own.shape[0] * far_re.shape[1], CHUNK)
        real = (own_re * far_re + own_im * far_im).astype(jnp.bfloat16).reshape(shape)
        imag = (own_im * far_re - own_re * far_im).astype(jnp.bfloat16).reshape(shape)
        term = dot(real, table_ref[re_cols, :]) + dot(imag, table_ref[im_cols, :])
        total = term if total is None else total + term
    return total.astype(jnp.bfloat16).reshape(own.shape[0], -1, LAGS)


def spectra_kernel(
    count,
    traces_hbm, live_hbm, segment_hbm, base_hbm, twiddle_hbm, table_hbm,
    rows_ref, part_ref,
    traces, live, segment, base, twiddle, table, first, second, spec, labels, whole,
    in_sem, here_sem, halo_send, halo_recv, row_send, row_recv,
):
    me = lax.axis_index("fiber")
    core = lax.rem(me, 2)
    depth = lax.rem(me // 2, 8)
    length = traces.shape[1]
    spans = -(-length // SPAN)

    barrier = pltpu.get_barrier_semaphore()

    def exists(step):
        return (me + step >= 0) & (me + step < count)

    def on(condition, action):
        pl.when(condition)(action)

    def signal(semaphore, step):
        pl.semaphore_signal(semaphore, inc=1, device_id=(me + step,), device_id_type=MESH)

    for step in (1, 2):
        on(exists(-step), functools.partial(signal, barrier, -step))

    small = [
        pltpu.make_async_copy(live_hbm, live, in_sem.at[0]),
        pltpu.make_async_copy(segment_hbm, segment, in_sem.at[1]),
        pltpu.make_async_copy(twiddle_hbm, twiddle, in_sem.at[2]),
    ]
    load_traces = pltpu.make_async_copy(traces_hbm, traces, in_sem.at[3])
    load_base = [pltpu.make_async_copy(base_hbm.at[c], base.at[c], in_sem.at[4 + c]) for c in range(CHUNKS)]
    load_table = pltpu.make_async_copy(table_hbm, table, in_sem.at[4 + CHUNKS])
    for load in (load_traces, *small, *load_base, load_table):
        load.start()

    def meet(slot):
        pl.semaphore_wait(here_sem.at[slot], 1)

    def greet():
        peers = sum(jnp.where(exists(step), 1, 0) for step in (1, 2))
        on(exists(1), lambda: pl.semaphore_wait(barrier, peers))
        for slot, step in enumerate((1, 2)):
            on(exists(step), functools.partial(signal, here_sem.at[slot], step))

    def relay():
        meet(1)
        on(exists(2), functools.partial(signal, here_sem.at[2], 2))

    last = depth == 7
    on(last, greet)

    whole[...] = jnp.zeros_like(whole)
    for load in small:
        load.wait()
    whole[0:1, 0:CH] = segment[...] * 2 + live[...]
    packed = whole[...]
    lane = lax.broadcasted_iota(jnp.int32, (8, 128), 1)
    labels[0] = pltpu.roll(packed, HALF, 1)
    labels[1] = jnp.where(lane < HALF, pltpu.roll(packed, 128 - HALF, 1), 0)
    labels[2] = jnp.where((lane >= CH + HALF) & (lane < CH + 2 * HALF), pltpu.roll(packed, CH + HALF, 1), 0)

    def remote(src, dst, send, recv, target):
        return pltpu.make_async_remote_copy(
            src_ref=src, dst_ref=dst, send_sem=send, recv_sem=recv, device_id=(target,), device_id_type=MESH
        )

    def halo(side, piece):
        target = me + 1 if side == 0 else me - 1
        send, recv = halo_send.at[side, piece], halo_recv.at[side, piece]
        if piece == CHUNKS:
            return remote(labels.at[1 + side], labels.at[3 + side], send, recv, target)
        cols = pl.ds(piece * WIDE, WIDE)
        source, place = ((CH, 0), (HALF, CH + HALF))[side]
        return remote(spec.at[pl.ds(source, HALF), cols], spec.at[pl.ds(place, HALF), cols], send, recv, target)

    on(last & exists(1), halo(0, CHUNKS).start)

    load_traces.wait()
    for s in range(spans):
        piece = traces[:, s * SPAN : min(length, (s + 1) * SPAN)]
        if piece.shape[1] < SPAN:
            piece = jnp.concatenate([piece, jnp.zeros((CH, SPAN - piece.shape[1]), jnp.float32)], axis=1)
        top = piece.astype(jnp.bfloat16)
        first[s * CH : (s + 1) * CH, :] = top
        second[s * CH : (s + 1) * CH, :] = (piece - top.astype(jnp.float32)).astype(jnp.bfloat16)
    for c in range(CHUNKS):
        load_base[c].wait()
        parts = []
        for offset in (0, CHUNK):
            cols = slice(offset, offset + CHUNK)
            high, low = base[c, 0, :, cols], base[c, 1, :, cols]
            parts.append(dot(first[...], high) + dot(second[...], high) + dot(first[...], low))
        cosine = twiddle[0:1, c * CHUNK : (c + 1) * CHUNK]
        sine = twiddle[1:2, c * CHUNK : (c + 1) * CHUNK]
        real = parts[0][(spans - 1) * CH :, :]
        imag = parts[1][(spans - 1) * CH :, :]
        for s in range(spans - 2, -1, -1):
            rows = slice(s * CH, (s + 1) * CH)
            real, imag = (
                parts[0][rows, :] + (real * cosine - imag * sine),
                parts[1][rows, :] + (real * sine + imag * cosine),
            )
        spec[HALF : HALF + CH, c * WIDE : c * WIDE + CHUNK] = real
        spec[HALF : HALF + CH, c * WIDE + CHUNK : (c + 1) * WIDE] = imag
        on(last & exists(1), halo(0, c).start)

    def open_right():
        greet()
        for piece in (CHUNKS, *range(CHUNKS)):
            on(exists(1), halo(0, piece).start)

    on(jnp.logical_not(last), open_right)

    on((depth > 0) & exists(-2), relay)

    def send_left():
        meet(0)
        for piece in (CHUNKS, *range(CHUNKS)):
            halo(1, piece).start()

    late = (depth == 0) & (core == 0)
    on(exists(-1) & jnp.logical_not(late), send_left)

    def row_slice(block, half):
        return rows_ref.at[pl.ds(block * CH + half * HALF, HALF)]

    def row_copy(kind, half, source, target_block, target):
        return remote(
            row_slice(source, half), row_slice(target_block, half),
            row_send.at[kind, half], row_recv.at[target_block - 1, half], target,
        )

    def to_sibling(half):
        return row_copy(0, half, 0, 1, me - 1)

    def to_two(half):
        return row_copy(1, half, 0, 2, me - 2)

    def to_four(half):
        return row_copy(2, half, 0, 4, me - 4)

    wide_row = lax.broadcasted_iota(jnp.int32, (CH, 128), 0) + HALF
    wide_lane = lax.broadcasted_iota(jnp.int32, (CH, 128), 1)
    near = jnp.abs(wide_lane - wide_row) <= HALF_WIN
    band_row = lax.broadcasted_iota(jnp.int32, (CHUNK, CHUNK), 0) // BAND
    band_col = lax.broadcasted_iota(jnp.int32, (CHUNK, CHUNK), 1) // BAND
    same = jnp.where(band_row == band_col, 1.0, 0.0).astype(jnp.bfloat16)

    def whiten(half):
        side = half
        there = exists(1) if half == 1 else exists(-1)
        edge = slice(CH + HALF, 2 * CH) if half == 1 else slice(0, HALF)

        def nobody():
            spec[edge, :] = jnp.zeros((HALF, 2 * FB), jnp.float32)
            labels[3 + side] = jnp.zeros((8, 128), jnp.int32)

        on(jnp.logical_not(there), nobody)
        on(there, halo(side, CHUNKS).wait_recv)
        low = half * HALF
        mine = jnp.where(wide_lane == wide_row, labels[0, 0:1, :], 0).astype(jnp.float32)
        mine = jnp.sum(mine, axis=1, keepdims=True).astype(jnp.int32)
        wide = labels[0, 0:1, :] + labels[3 + side, 0:1, :]
        keep = near & ((wide >> 1) == (mine >> 1)) & ((wide & 1) == 1)
        inside = jnp.where(keep, 1.0, 0.0)
        divisor = jnp.maximum(jnp.sum(inside, axis=1, keepdims=True), 1.0)[low : low + HALF]
        alive = (mine & 1).astype(jnp.float32)[low : low + HALF]
        weights = inside[low : low + HALF, low : low + 3 * HALF].astype(jnp.bfloat16)
        weights = jnp.concatenate([weights, weights, weights], axis=1)
        for c in range(CHUNKS):
            on(there, halo(side, c).wait_recv)
            parts = []
            for offset in (c * WIDE, c * WIDE + CHUNK):
                cols = slice(offset, offset + CHUNK)
                stack = jnp.concatenate(split3(spec[low : low + 3 * HALF, cols]), axis=0)
                total = dot(weights, stack)
                value = spec[HALF + low : 2 * HALF + low, cols]
                parts.append(alive * (value * alive - total / divisor))
            square = parts[0] * parts[0] + parts[1] * parts[1]
            sums = dot(jnp.concatenate(split3(square), axis=0), same)
            power = (sums[:HALF] + (sums[HALF : 2 * HALF] + sums[2 * HALF :])) * (1.0 / BAND)
            scale = lax.rsqrt(power + WHITEN_EPS)
            rows_ref[low : low + HALF, c * WIDE : c * WIDE + CHUNK] = (parts[0] * scale).astype(jnp.bfloat16)
            rows_ref[low : low + HALF, c * WIDE + CHUNK : (c + 1) * WIDE] = (parts[1] * scale).astype(jnp.bfloat16)

    def blank(block):
        rows_ref[block * CH : (block + 1) * CH, :] = jnp.zeros((CH, 2 * FB), jnp.bfloat16)

    for block in range(1, REACH + 1):
        on(jnp.logical_not(exists(block)), functools.partial(blank, block))

    def send_early(half):
        on(core == 1, to_sibling(half).start)
        on((depth > 0) & exists(-2), to_two(half).start)
        if half == 1:
            on((depth > 1) & exists(-4), lambda: meet(2))
        on((depth > 1) & exists(-4), to_four(half).start)

    def lower():
        whiten(0)
        send_early(0)

    whiten(1)
    send_early(1)
    on(jnp.logical_not(late), lower)

    def arrived(block, half):
        row_copy(0, half, 0, block, me).wait_recv()

    passed = []

    def forward(block):
        for half in (1, 0):
            on(exists(block), functools.partial(arrived, block, half))
            kind = 3 if block == 2 else 4
            to_low_core_next = row_copy(kind, half, block, block - 1, me + 1)
            on(exists(block) & (core == 0), to_low_core_next.start)
            if block == 2:
                on(exists(block) & (core == 1), row_copy(kind, half, block, 3, me - 1).start)
                passed.append((to_low_core_next, exists(block)))
            else:
                passed.append((to_low_core_next, exists(block) & (core == 0)))

    own = rows_ref[HALF:CH, :].astype(jnp.float32)

    def correlate_upper(block):
        rows = slice(block * CH, (block + 2) * CH)
        for g in range(0, HALF, 16):
            part_ref[g : g + 16, (block - 1) * CH : (block + 1) * CH, :] = correlate(
                own[g : g + 16], lambda cols: rows_ref[rows, cols], table
            )

    forward(2)
    for half in (1, 0):
        on(exists(1), functools.partial(arrived, 1, half))
    load_table.wait()
    correlate_upper(1)

    def catch_up():
        on((depth == 0) & exists(-2), relay)
        on(exists(-4), lambda: meet(2))
        for half in (1, 0):
            @pl.when((half == 1) | jnp.logical_not(late))
            def _():
                on((depth == 0) & exists(-2), to_two(half).start)
                on(exists(-4), to_four(half).start)

    on(exists(-1) & late, send_left)
    on(depth <= 1, catch_up)
    forward(4)
    for half in (1, 0):
        on(exists(3), functools.partial(arrived, 3, half))
    correlate_upper(3)

    def late_lower():
        whiten(0)
        on(exists(-2), to_two(0).start)
        on(exists(-4), to_four(0).start)

    on(late, late_lower)

    for side in (0, 1):
        for piece in range(CHUNKS + 1):
            on(exists(1 - 2 * side), halo(side, piece).wait_send)
    for half in (1, 0):
        on(core == 1, to_sibling(half).wait_send)
        on(exists(-2), to_two(half).wait_send)
        on(exists(-4), to_four(half).wait_send)
    for copy, condition in passed:
        on(condition, copy.wait_send)


GROUP = 8


def finish_kernel(rows_ref, part_ref, table_ref, out_ref):
    step = pl.program_id(0)

    @pl.when(step == 0)
    def _():
        out_ref[...] = part_ref[0:GROUP]

    @pl.when(step == 1)
    def _():
        out_ref[...] = part_ref[GROUP:HALF]

    @pl.when(step >= 2)
    def _():
        own = rows_ref[0:HALF, :].astype(jnp.float32)
        own = jnp.where(step == 2, own[:GROUP], own[GROUP:])
        out_ref[...] = correlate(own, lambda cols: rows_ref[CH:, cols], table_ref)


def on_device(traces, live, segment):
    count = lax.axis_size("fiber")
    channels, length = traces.shape
    base, twiddle, lags = (jnp.asarray(t) for t in tables(length))
    in_hbm = pl.BlockSpec(memory_space=pltpu.HBM)
    in_vmem = pl.BlockSpec(memory_space=pltpu.VMEM)
    spans = -(-length // SPAN)
    rows, part = pl.pallas_call(
        functools.partial(spectra_kernel, count),
        out_shape=(
            jax.ShapeDtypeStruct(((1 + REACH) * channels, 2 * FB), jnp.bfloat16),
            jax.ShapeDtypeStruct((HALF, REACH * channels, LAGS), jnp.bfloat16),
        ),
        in_specs=[in_hbm] * 6,
        out_specs=(in_vmem, in_vmem),
        scratch_shapes=[
            pltpu.VMEM((channels, length), jnp.float32),
            pltpu.VMEM((1, channels), jnp.int32),
            pltpu.VMEM((1, channels), jnp.int32),
            pltpu.VMEM((CHUNKS, 2, SPAN, WIDE), jnp.bfloat16),
            pltpu.VMEM((2, FB), jnp.float32),
            pltpu.VMEM((2 * FB, LAGS), jnp.bfloat16),
            pltpu.VMEM((spans * CH, SPAN), jnp.bfloat16),
            pltpu.VMEM((spans * CH, SPAN), jnp.bfloat16),
            pltpu.VMEM((2 * CH, 2 * FB), jnp.float32),
            pltpu.VMEM((5, 8, 128), jnp.int32),
            pltpu.VMEM((8, 128), jnp.int32),
            pltpu.SemaphoreType.DMA((5 + CHUNKS,)),
            pltpu.SemaphoreType.REGULAR((3,)),
            pltpu.SemaphoreType.DMA((2, CHUNKS + 1)),
            pltpu.SemaphoreType.DMA((2, CHUNKS + 1)),
            pltpu.SemaphoreType.DMA((5, 2)),
            pltpu.SemaphoreType.DMA((4, 2)),
        ],
        compiler_params=pltpu.CompilerParams(
            collective_id=0, has_side_effects=True, vmem_limit_bytes=40 * 1024 * 1024
        ),
        name="spectra",
    )(
        *(
            pltpu.with_memory_space_constraint(x, pltpu.HBM)
            for x in (traces, live.reshape(1, channels), segment.reshape(1, channels), base, twiddle, lags)
        )
    )
    return pl.pallas_call(
        finish_kernel,
        grid=(channels // GROUP,),
        out_shape=jax.ShapeDtypeStruct((channels, REACH * channels, LAGS), jnp.bfloat16),
        in_specs=[in_vmem] * 3,
        out_specs=pl.BlockSpec((GROUP, REACH * channels, LAGS), lambda g: (lax.rem(g + 2, 4), 0, 0)),
        compiler_params=pltpu.CompilerParams(vmem_limit_bytes=40 * 1024 * 1024),
        name="finish",
    )(rows, part, lags)


def solution(mesh):
    return jax.shard_map(
        on_device,
        mesh=mesh,
        in_specs=(P("fiber", None), P("fiber"), P("fiber")),
        out_specs=P("fiber", None, None),
        check_vma=False,
    )
```

```python
import functools
import math

import jax
import jax.numpy as jnp
import ml_dtypes
import numpy as np
from jax import lax
from jax.experimental import pallas as pl
from jax.experimental.pallas import tpu as pltpu
from jax.sharding import PartitionSpec as P

LOW_BIN = 32
FB = 768
BAND = 64
HALF_WIN = 15
LAGS = 256
CH = 32
HALF = 16
REACH = 4
SPAN = 256
CHUNK = 256
WHITEN_EPS = 1.0
MESH = pl.DeviceIdType.MESH


CHUNKS = FB // CHUNK
WIDE = 2 * CHUNK


def chunk_major(table, axis):
    halves = np.split(table, 2, axis=axis)
    pieces = [np.split(half, CHUNKS, axis=axis) for half in halves]
    return [np.concatenate([pieces[0][c], pieces[1][c]], axis=axis) for c in range(CHUNKS)]


def tables(length):
    bins = LOW_BIN + np.arange(FB)
    taper = np.sin(np.pi * (np.arange(FB) + 0.5) / FB)
    angle = 2.0 * np.pi / length * np.mod(np.arange(SPAN)[:, None] * bins[None, :], length)
    base = np.concatenate([np.cos(angle) * taper, -np.sin(angle) * taper], axis=1)
    base = np.stack(chunk_major(base, 1))
    high = base.astype(ml_dtypes.bfloat16)
    low = (base - high.astype(np.float64)).astype(ml_dtypes.bfloat16)
    turn = 2.0 * np.pi / length * np.mod(SPAN * bins, length)
    twiddle = np.stack([np.cos(turn), -np.sin(turn)]).astype(np.float32)
    lag = np.arange(LAGS) - LAGS // 2
    phase = 2.0 * np.pi / length * np.mod(bins[:, None] * lag[None, :], length)
    lags = np.concatenate([np.cos(phase), -np.sin(phase)], axis=0) / math.sqrt(FB)
    lags = np.concatenate(chunk_major(lags.astype(np.float32), 0), axis=0)
    return np.stack([high, low], axis=1), twiddle, lags.astype(ml_dtypes.bfloat16)


def split3(value):
    first = value.astype(jnp.bfloat16)
    rest = value - first.astype(jnp.float32)
    second = rest.astype(jnp.bfloat16)
    third = (rest - second.astype(jnp.float32)).astype(jnp.bfloat16)
    return first, second, third


def dot(a, b):
    return jnp.dot(a, b, preferred_element_type=jnp.float32)


def columns(start, width=CHUNK):
    return pl.ds(start if isinstance(start, int) else pl.multiple_of(start, CHUNK), width)


def correlate(own, far, table_ref, shape):
    total = None
    for c in range(CHUNKS):
        re_cols = slice(c * WIDE, c * WIDE + CHUNK)
        im_cols = slice(c * WIDE + CHUNK, (c + 1) * WIDE)
        own_re = own(re_cols)[:, None]
        own_im = own(im_cols)[:, None]
        far_re = far(re_cols).astype(jnp.float32)[None]
        far_im = far(im_cols).astype(jnp.float32)[None]
        flat = (own_re.shape[0] * far_re.shape[1], CHUNK)
        real = (own_re * far_re + own_im * far_im).astype(jnp.bfloat16).reshape(flat)
        imag = (own_im * far_re - own_re * far_im).astype(jnp.bfloat16).reshape(flat)
        term = dot(real, table_ref[re_cols, :]) + dot(imag, table_ref[im_cols, :])
        total = term if total is None else total + term
    return total.astype(jnp.bfloat16).reshape(shape)


def spectra_kernel(
    count,
    traces_hbm, live_hbm, segment_hbm, base_hbm, twiddle_hbm, table_hbm,
    rows_ref, part_ref,
    traces, live, segment, base, twiddle, table, first, second, spec, labels, whole, own,
    in_sem, here_sem, halo_send, halo_recv, row_send, row_recv,
):
    me = lax.axis_index("fiber")
    core = lax.rem(me, 2)
    depth = lax.rem(me // 2, 8)
    length = traces.shape[1]
    spans = -(-length // SPAN)

    barrier = pltpu.get_barrier_semaphore()

    def exists(step):
        return (me + step >= 0) & (me + step < count)

    def on(condition, action):
        pl.when(condition)(action)

    def signal(semaphore, step):
        pl.semaphore_signal(semaphore, inc=1, device_id=(me + step,), device_id_type=MESH)

    for step in (1, 2):
        on(exists(-step), functools.partial(signal, barrier, -step))

    small = [
        pltpu.make_async_copy(live_hbm, live, in_sem.at[0]),
        pltpu.make_async_copy(segment_hbm, segment, in_sem.at[1]),
        pltpu.make_async_copy(twiddle_hbm, twiddle, in_sem.at[2]),
    ]
    load_traces = pltpu.make_async_copy(traces_hbm, traces, in_sem.at[3])
    load_base = [pltpu.make_async_copy(base_hbm.at[c], base.at[c], in_sem.at[4 + c]) for c in range(CHUNKS)]
    load_table = pltpu.make_async_copy(table_hbm, table, in_sem.at[4 + CHUNKS])
    for load in (load_traces, *small, *load_base, load_table):
        load.start()

    def meet(slot):
        pl.semaphore_wait(here_sem.at[slot], 1)

    def greet():
        peers = sum(jnp.where(exists(step), 1, 0) for step in (1, 2))
        on(exists(1), lambda: pl.semaphore_wait(barrier, peers))
        for slot, step in enumerate((1, 2)):
            on(exists(step), functools.partial(signal, here_sem.at[slot], step))

    def relay():
        meet(1)
        on(exists(2), functools.partial(signal, here_sem.at[2], 2))

    last = depth == 7
    on(last, greet)

    whole[...] = jnp.zeros_like(whole)
    for load in small:
        load.wait()
    whole[0:1, 0:CH] = segment[...] * 2 + live[...]
    packed = whole[...]
    lane = lax.broadcasted_iota(jnp.int32, (8, 128), 1)
    labels[0] = pltpu.roll(packed, HALF, 1)
    labels[1] = jnp.where(lane < HALF, pltpu.roll(packed, 128 - HALF, 1), 0)
    labels[2] = jnp.where((lane >= CH + HALF) & (lane < CH + 2 * HALF), pltpu.roll(packed, CH + HALF, 1), 0)

    def remote(src, dst, send, recv, target):
        return pltpu.make_async_remote_copy(
            src_ref=src, dst_ref=dst, send_sem=send, recv_sem=recv, device_id=(target,), device_id_type=MESH
        )

    def halo(side, piece):
        target = me + 1 if side == 0 else me - 1
        send, recv = halo_send.at[side, piece], halo_recv.at[side, piece]
        if isinstance(piece, int) and piece == CHUNKS:
            return remote(labels.at[1 + side], labels.at[3 + side], send, recv, target)
        cols = columns(piece * WIDE, WIDE)
        source, place = ((CH, 0), (HALF, CH + HALF))[side]
        return remote(spec.at[pl.ds(source, HALF), cols], spec.at[pl.ds(place, HALF), cols], send, recv, target)

    on(last & exists(1), halo(0, CHUNKS).start)

    load_traces.wait()
    for s in range(spans):
        piece = traces[:, s * SPAN : min(length, (s + 1) * SPAN)]
        if piece.shape[1] < SPAN:
            piece = jnp.concatenate([piece, jnp.zeros((CH, SPAN - piece.shape[1]), jnp.float32)], axis=1)
        top = piece.astype(jnp.bfloat16)
        first[s * CH : (s + 1) * CH, :] = top
        second[s * CH : (s + 1) * CH, :] = (piece - top.astype(jnp.float32)).astype(jnp.bfloat16)

    def transform(c, carry):
        pltpu.make_async_copy(base_hbm.at[c], base.at[c], in_sem.at[4 + c]).wait()
        parts = []
        for offset in (0, CHUNK):
            high, low = (base[c, k, :, offset : offset + CHUNK] for k in (0, 1))
            parts.append(dot(first[...], high) + dot(second[...], high) + dot(first[...], low))
        cosine = twiddle[0:1, columns(c * CHUNK)]
        sine = twiddle[1:2, columns(c * CHUNK)]
        real = parts[0][(spans - 1) * CH :, :]
        imag = parts[1][(spans - 1) * CH :, :]
        for s in range(spans - 2, -1, -1):
            rows = slice(s * CH, (s + 1) * CH)
            real, imag = (
                parts[0][rows, :] + (real * cosine - imag * sine),
                parts[1][rows, :] + (real * sine + imag * cosine),
            )
        spec[HALF : HALF + CH, columns(c * WIDE)] = real
        spec[HALF : HALF + CH, columns(c * WIDE + CHUNK)] = imag
        on(last & exists(1), halo(0, c).start)
        return carry

    lax.fori_loop(0, CHUNKS, transform, 0)

    def open_right():
        greet()
        for piece in (CHUNKS, *range(CHUNKS)):
            on(exists(1), halo(0, piece).start)

    on(jnp.logical_not(last), open_right)

    on((depth > 0) & exists(-2), relay)

    def send_left():
        meet(0)
        for piece in (CHUNKS, *range(CHUNKS)):
            halo(1, piece).start()

    late = (depth == 0) & (core == 0)
    on(exists(-1) & jnp.logical_not(late), send_left)

    def row_slice(block, half):
        return rows_ref.at[pl.ds(block * CH + half * HALF, HALF)]

    def row_copy(kind, half, source, target_block, target):
        return remote(
            row_slice(source, half), row_slice(target_block, half),
            row_send.at[kind, half], row_recv.at[target_block - 1, half], target,
        )

    def to_sibling(half):
        return row_copy(0, half, 0, 1, me - 1)

    def to_two(half):
        return row_copy(1, half, 0, 2, me - 2)

    def to_four(half):
        return row_copy(2, half, 0, 4, me - 4)

    wide_row = lax.broadcasted_iota(jnp.int32, (HALF, 128), 0) + HALF
    wide_lane = lax.broadcasted_iota(jnp.int32, (HALF, 128), 1)
    band_row = lax.broadcasted_iota(jnp.int32, (CHUNK, CHUNK), 0) // BAND
    band_col = lax.broadcasted_iota(jnp.int32, (CHUNK, CHUNK), 1) // BAND

    def whiten(half):
        there = ((half == 1) & exists(1)) | ((half == 0) & exists(-1))
        low = pl.multiple_of(half * HALF, HALF)

        @pl.when(there)
        def _():
            for piece in (CHUNKS, *range(CHUNKS)):
                on(half == 0, halo(0, piece).wait_recv)
                on(half == 1, halo(1, piece).wait_recv)

        @pl.when(jnp.logical_not(there))
        def _():
            spec[pl.ds(pl.multiple_of(half * (CH + HALF), HALF), HALF), :] = jnp.zeros((HALF, 2 * FB), jnp.float32)
            labels[3 + half] = jnp.zeros((8, 128), jnp.int32)

        place = wide_row + low
        mine = jnp.where(wide_lane == place, labels[0, 0:1, :], 0).astype(jnp.float32)
        mine = jnp.sum(mine, axis=1, keepdims=True).astype(jnp.int32)
        wide = labels[0, 0:1, :] + labels[3 + half, 0:1, :]
        keep = (jnp.abs(wide_lane - place) <= HALF_WIN) & ((wide >> 1) == (mine >> 1)) & ((wide & 1) == 1)
        inside = jnp.where(keep, 1.0, 0.0)
        divisor = jnp.maximum(jnp.sum(inside, axis=1, keepdims=True), 1.0)
        alive = (mine & 1).astype(jnp.float32)
        weights = jnp.where(half == 1, pltpu.roll(inside, 128 - HALF, 1), inside)[:, : 3 * HALF].astype(jnp.bfloat16)
        weights = jnp.concatenate([weights, weights, weights], axis=1)
        same = jnp.where(band_row == band_col, 1.0, 0.0).astype(jnp.bfloat16)
        for c in range(CHUNKS):
            parts = []
            for offset in (c * WIDE, c * WIDE + CHUNK):
                cols = slice(offset, offset + CHUNK)
                stack = jnp.concatenate(split3(spec[pl.ds(low, 3 * HALF), cols]), axis=0)
                sums = dot(weights, stack)
                value = spec[pl.ds(pl.multiple_of(HALF + low, HALF), HALF), cols]
                parts.append(alive * (value * alive - sums / divisor))
            square = parts[0] * parts[0] + parts[1] * parts[1]
            sums = dot(jnp.concatenate(split3(square), axis=0), same)
            power = (sums[:HALF] + (sums[HALF : 2 * HALF] + sums[2 * HALF :])) * (1.0 / BAND)
            scale = lax.rsqrt(power + WHITEN_EPS)
            rows_ref[pl.ds(low, HALF), c * WIDE : c * WIDE + CHUNK] = (parts[0] * scale).astype(jnp.bfloat16)
            rows_ref[pl.ds(low, HALF), c * WIDE + CHUNK : (c + 1) * WIDE] = (parts[1] * scale).astype(jnp.bfloat16)

    def blank(block):
        rows_ref[block * CH : (block + 1) * CH, :] = jnp.zeros((CH, 2 * FB), jnp.bfloat16)

    for block in range(1, REACH + 1):
        on(jnp.logical_not(exists(block)), functools.partial(blank, block))

    def arrived(block, half):
        row_copy(0, half, 0, block, me).wait_recv()

    def to_next(block, half):
        return row_copy(3 if block == 2 else 4, half, block, block - 1, me + 1)

    def forward(block):
        for half in (1, 0):
            on(exists(block), functools.partial(arrived, block, half))
            on(exists(block) & (core == 0), to_next(block, half).start)
            if block == 2:
                on(exists(block) & (core == 1), row_copy(3, half, block, 3, me - 1).start)

    def catch_up():
        on((depth == 0) & exists(-2), relay)
        on(exists(-4), lambda: meet(2))
        for half in (1, 0):
            @pl.when((half == 1) | jnp.logical_not(late))
            def _():
                on((depth == 0) & exists(-2), to_two(half).start)
                on(exists(-4), to_four(half).start)

    def stage(t, carry):
        @pl.when((t == 0) | ((t == 1) & jnp.logical_not(late)) | ((t == 4) & late))
        def _():
            half = jnp.where(t == 0, 1, 0)
            whiten(half)
            on(core == 1, to_sibling(half).start)
            on(((depth > 0) | (t == 4)) & exists(-2), to_two(half).start)
            on((depth > 1) & (t == 0) & exists(-4), lambda: meet(2))
            on(((depth > 1) | (t == 4)) & exists(-4), to_four(half).start)

        @pl.when((t == 2) | (t == 3))
        def _():
            @pl.when(t == 2)
            def _():
                forward(2)
                for half in (1, 0):
                    on(exists(1), functools.partial(arrived, 1, half))
                load_table.wait()
                own[...] = rows_ref[HALF:CH, :].astype(jnp.float32)

            @pl.when(t == 3)
            def _():
                on(exists(-1) & late, send_left)
                on(depth <= 1, catch_up)
                forward(4)
                for half in (1, 0):
                    on(exists(3), functools.partial(arrived, 3, half))

            pair = t - 2
            far_rows = pl.ds(pl.multiple_of(CH + pair * 2 * CH, CH), 2 * CH)
            part_ref[:, pl.ds(pl.multiple_of(pair * 2 * CH, CH), 2 * CH), :] = correlate(
                lambda cols: own[:, cols], lambda cols: rows_ref[far_rows, cols], table, (HALF, 2 * CH, LAGS)
            )

        return carry

    lax.fori_loop(0, 5, stage, 0)

    for side in (0, 1):
        for piece in range(CHUNKS + 1):
            on(exists(1 - 2 * side), halo(side, piece).wait_send)
    for half in (1, 0):
        on(core == 1, to_sibling(half).wait_send)
        on(exists(-2), to_two(half).wait_send)
        on(exists(-4), to_four(half).wait_send)
    for half in (1, 0):
        on(exists(2), to_next(2, half).wait_send)
        on(exists(4) & (core == 0), to_next(4, half).wait_send)


GROUP = 8


def finish_kernel(rows_ref, part_ref, table_ref, out_ref, own, done, sem):
    upper = pltpu.make_async_copy(part_ref, out_ref.at[pl.ds(HALF, HALF)], sem.at[0])
    upper.start()
    own[...] = rows_ref[0:HALF, :].astype(jnp.float32)

    def lower(p):
        rows = pl.ds(pl.multiple_of(p * GROUP, GROUP), GROUP)
        return rows, pltpu.make_async_copy(done.at[rows], out_ref.at[rows], sem.at[1 + p])

    def step(p, carry):
        rows, copy = lower(p)
        done[rows] = correlate(
            lambda cols: own[rows, cols], lambda cols: rows_ref[CH:, cols], table_ref, (GROUP, REACH * CH, LAGS)
        )
        copy.start()
        return carry

    lax.fori_loop(0, HALF // GROUP, step, 0)
    upper.wait()
    for p in range(HALF // GROUP):
        lower(p)[1].wait()


def on_device(traces, live, segment):
    count = lax.axis_size("fiber")
    channels, length = traces.shape
    base, twiddle, lags = (jnp.asarray(t) for t in tables(length))
    in_hbm = pl.BlockSpec(memory_space=pltpu.HBM)
    in_vmem = pl.BlockSpec(memory_space=pltpu.VMEM)
    spans = -(-length // SPAN)
    rows, part = pl.pallas_call(
        functools.partial(spectra_kernel, count),
        out_shape=(
            jax.ShapeDtypeStruct(((1 + REACH) * channels, 2 * FB), jnp.bfloat16),
            jax.ShapeDtypeStruct((HALF, REACH * channels, LAGS), jnp.bfloat16),
        ),
        in_specs=[in_hbm] * 6,
        out_specs=(in_vmem, in_vmem),
        scratch_shapes=[
            pltpu.VMEM((channels, length), jnp.float32),
            pltpu.VMEM((1, channels), jnp.int32),
            pltpu.VMEM((1, channels), jnp.int32),
            pltpu.VMEM((CHUNKS, 2, SPAN, WIDE), jnp.bfloat16),
            pltpu.VMEM((2, FB), jnp.float32),
            pltpu.VMEM((2 * FB, LAGS), jnp.bfloat16),
            pltpu.VMEM((spans * CH, SPAN), jnp.bfloat16),
            pltpu.VMEM((spans * CH, SPAN), jnp.bfloat16),
            pltpu.VMEM((2 * CH, 2 * FB), jnp.float32),
            pltpu.VMEM((5, 8, 128), jnp.int32),
            pltpu.VMEM((8, 128), jnp.int32),
            pltpu.VMEM((HALF, 2 * FB), jnp.float32),
            pltpu.SemaphoreType.DMA((5 + CHUNKS,)),
            pltpu.SemaphoreType.REGULAR((3,)),
            pltpu.SemaphoreType.DMA((2, CHUNKS + 1)),
            pltpu.SemaphoreType.DMA((2, CHUNKS + 1)),
            pltpu.SemaphoreType.DMA((5, 2)),
            pltpu.SemaphoreType.DMA((4, 2)),
        ],
        compiler_params=pltpu.CompilerParams(
            collective_id=0, has_side_effects=True, vmem_limit_bytes=40 * 1024 * 1024
        ),
        name="spectra",
    )(
        *(
            pltpu.with_memory_space_constraint(x, pltpu.HBM)
            for x in (traces, live.reshape(1, channels), segment.reshape(1, channels), base, twiddle, lags)
        )
    )
    return pl.pallas_call(
        finish_kernel,
        out_shape=jax.ShapeDtypeStruct((channels, REACH * channels, LAGS), jnp.bfloat16),
        in_specs=[in_vmem] * 3,
        out_specs=in_hbm,
        scratch_shapes=[
            pltpu.VMEM((HALF, 2 * FB), jnp.float32),
            pltpu.VMEM((HALF, REACH * CH, LAGS), jnp.bfloat16),
            pltpu.SemaphoreType.DMA((1 + HALF // GROUP,)),
        ],
        compiler_params=pltpu.CompilerParams(vmem_limit_bytes=40 * 1024 * 1024),
        name="finish",
    )(rows, part, lags)


def solution(mesh):
    return jax.shard_map(
        on_device,
        mesh=mesh,
        in_specs=(P("fiber", None), P("fiber"), P("fiber")),
        out_specs=P("fiber", None, None),
        check_vma=False,
    )
```

```python
import functools
import math

import jax
import jax.numpy as jnp
import ml_dtypes
import numpy as np
from jax import lax
from jax.experimental import pallas as pl
from jax.experimental.pallas import tpu as pltpu
from jax.sharding import PartitionSpec as P

LOW_BIN = 32
FB = 768
BAND = 64
HALF_WIN = 15
LAGS = 256
CH = 32
HALF = 16
REACH = 4
SPAN = 256
CHUNK = 256
WHITEN_EPS = 1.0
MESH = pl.DeviceIdType.MESH


CHUNKS = FB // CHUNK
WIDE = 2 * CHUNK


def chunk_major(table, axis):
    halves = np.split(table, 2, axis=axis)
    pieces = [np.split(half, CHUNKS, axis=axis) for half in halves]
    return [np.concatenate([pieces[0][c], pieces[1][c]], axis=axis) for c in range(CHUNKS)]


def tables(length):
    bins = LOW_BIN + np.arange(FB)
    taper = np.sin(np.pi * (np.arange(FB) + 0.5) / FB)
    angle = 2.0 * np.pi / length * np.mod(np.arange(SPAN)[:, None] * bins[None, :], length)
    base = np.concatenate([np.cos(angle) * taper, -np.sin(angle) * taper], axis=1)
    base = np.stack(chunk_major(base, 1))
    high = base.astype(ml_dtypes.bfloat16)
    low = (base - high.astype(np.float64)).astype(ml_dtypes.bfloat16)
    turn = 2.0 * np.pi / length * np.mod(SPAN * bins, length)
    twiddle = np.stack([np.cos(turn), -np.sin(turn)]).astype(np.float32)
    lag = np.arange(LAGS) - LAGS // 2
    phase = 2.0 * np.pi / length * np.mod(bins[:, None] * lag[None, :], length)
    lags = np.concatenate([np.cos(phase), -np.sin(phase)], axis=0) / math.sqrt(FB)
    lags = np.concatenate(chunk_major(lags.astype(np.float32), 0), axis=0)
    return np.stack([high, low], axis=1), twiddle, lags.astype(ml_dtypes.bfloat16)


def split3(value):
    first = value.astype(jnp.bfloat16)
    rest = value - first.astype(jnp.float32)
    second = rest.astype(jnp.bfloat16)
    third = (rest - second.astype(jnp.float32)).astype(jnp.bfloat16)
    return first, second, third


def dot(a, b):
    return jnp.dot(a, b, preferred_element_type=jnp.float32)


def columns(start, width=CHUNK):
    return pl.ds(start if isinstance(start, int) else pl.multiple_of(start, CHUNK), width)


def correlate(own, far, table_ref, shape):
    total = None
    for c in range(CHUNKS):
        re_cols = slice(c * WIDE, c * WIDE + CHUNK)
        im_cols = slice(c * WIDE + CHUNK, (c + 1) * WIDE)
        own_re = own(re_cols)[:, None]
        own_im = own(im_cols)[:, None]
        far_re = far(re_cols).astype(jnp.float32)[None]
        far_im = far(im_cols).astype(jnp.float32)[None]
        flat = (own_re.shape[0] * far_re.shape[1], CHUNK)
        real = (own_re * far_re + own_im * far_im).astype(jnp.bfloat16).reshape(flat)
        imag = (own_im * far_re - own_re * far_im).astype(jnp.bfloat16).reshape(flat)
        term = dot(real, table_ref[re_cols, :]) + dot(imag, table_ref[im_cols, :])
        total = term if total is None else total + term
    return total.astype(jnp.bfloat16).reshape(shape)


def spectra_kernel(
    count,
    traces_hbm, live_hbm, segment_hbm, base_hbm, twiddle_hbm, table_hbm,
    rows_ref, part_ref,
    traces, live, segment, base, twiddle, table, first, second, spec, labels, whole, own,
    in_sem, here_sem, halo_send, halo_recv, row_send, row_recv,
):
    me = lax.axis_index("fiber")
    core = lax.rem(me, 2)
    depth = lax.rem(me // 2, 8)
    length = traces.shape[1]
    spans = -(-length // SPAN)

    barrier = pltpu.get_barrier_semaphore()

    def exists(step):
        return (me + step >= 0) & (me + step < count)

    def on(condition, action):
        pl.when(condition)(action)

    def signal(semaphore, step):
        pl.semaphore_signal(semaphore, inc=1, device_id=(me + step,), device_id_type=MESH)

    for step in (1, 2):
        on(exists(-step), functools.partial(signal, barrier, -step))
    on((depth < 7) & exists(2), functools.partial(signal, barrier, 2))

    small = [
        pltpu.make_async_copy(live_hbm, live, in_sem.at[0]),
        pltpu.make_async_copy(segment_hbm, segment, in_sem.at[1]),
        pltpu.make_async_copy(twiddle_hbm, twiddle, in_sem.at[2]),
    ]
    load_traces = pltpu.make_async_copy(traces_hbm, traces, in_sem.at[3])
    load_base = [pltpu.make_async_copy(base_hbm.at[c], base.at[c], in_sem.at[4 + c]) for c in range(CHUNKS)]
    load_table = pltpu.make_async_copy(table_hbm, table, in_sem.at[4 + CHUNKS])
    for load in (load_traces, *small, *load_base, load_table):
        load.start()

    def meet(slot):
        pl.semaphore_wait(here_sem.at[slot], 1)

    def greet():
        awaited = (exists(1), exists(2), (depth > 0) & exists(-2))
        peers = sum(jnp.where(peer, 1, 0) for peer in awaited)
        on(peers > 0, lambda: pl.semaphore_wait(barrier, peers))
        on(exists(1), functools.partial(signal, here_sem.at[0], 1))
        on((depth == 7) & exists(2), functools.partial(signal, here_sem.at[1], 2))
        on(depth > 0, relay)

    def relay():
        on(exists(-2) & exists(2), functools.partial(signal, here_sem.at[2], 2))

    last = depth == 7

    whole[...] = jnp.zeros_like(whole)
    for load in small:
        load.wait()
    whole[0:1, 0:CH] = segment[...] * 2 + live[...]
    packed = whole[...]
    lane = lax.broadcasted_iota(jnp.int32, (8, 128), 1)
    labels[0] = pltpu.roll(packed, HALF, 1)
    labels[1] = jnp.where(lane < HALF, pltpu.roll(packed, 128 - HALF, 1), 0)
    labels[2] = jnp.where((lane >= CH + HALF) & (lane < CH + 2 * HALF), pltpu.roll(packed, CH + HALF, 1), 0)

    def remote(src, dst, send, recv, target):
        return pltpu.make_async_remote_copy(
            src_ref=src, dst_ref=dst, send_sem=send, recv_sem=recv, device_id=(target,), device_id_type=MESH
        )

    def halo(side, piece):
        target = me + 1 if side == 0 else me - 1
        send, recv = halo_send.at[side, piece], halo_recv.at[side, piece]
        if isinstance(piece, int) and piece == CHUNKS:
            return remote(labels.at[1 + side], labels.at[3 + side], send, recv, target)
        cols = columns(piece * WIDE, WIDE)
        source, place = ((CH, 0), (HALF, CH + HALF))[side]
        return remote(spec.at[pl.ds(source, HALF), cols], spec.at[pl.ds(place, HALF), cols], send, recv, target)

    load_traces.wait()
    for s in range(spans):
        piece = traces[:, s * SPAN : min(length, (s + 1) * SPAN)]
        if piece.shape[1] < SPAN:
            piece = jnp.concatenate([piece, jnp.zeros((CH, SPAN - piece.shape[1]), jnp.float32)], axis=1)
        top = piece.astype(jnp.bfloat16)
        first[s * CH : (s + 1) * CH, :] = top
        second[s * CH : (s + 1) * CH, :] = (piece - top.astype(jnp.float32)).astype(jnp.bfloat16)

    def greet_first():
        greet()
        on(exists(1), halo(0, CHUNKS).start)

    on(last, greet_first)

    def transform(c, carry):
        pltpu.make_async_copy(base_hbm.at[c], base.at[c], in_sem.at[4 + c]).wait()
        parts = []
        for offset in (0, CHUNK):
            high, low = (base[c, k, :, offset : offset + CHUNK] for k in (0, 1))
            parts.append(dot(first[...], high) + dot(second[...], high) + dot(first[...], low))
        cosine = twiddle[0:1, columns(c * CHUNK)]
        sine = twiddle[1:2, columns(c * CHUNK)]
        real = parts[0][(spans - 1) * CH :, :]
        imag = parts[1][(spans - 1) * CH :, :]
        for s in range(spans - 2, -1, -1):
            rows = slice(s * CH, (s + 1) * CH)
            real, imag = (
                parts[0][rows, :] + (real * cosine - imag * sine),
                parts[1][rows, :] + (real * sine + imag * cosine),
            )
        spec[HALF : HALF + CH, columns(c * WIDE)] = real
        spec[HALF : HALF + CH, columns(c * WIDE + CHUNK)] = imag
        on(last & exists(1), halo(0, c).start)
        return carry

    lax.fori_loop(0, CHUNKS, transform, 0)

    def open_right():
        greet()
        for piece in (CHUNKS, *range(CHUNKS)):
            on(exists(1), halo(0, piece).start)

    on(jnp.logical_not(last), open_right)

    def send_left():
        meet(0)
        for piece in (CHUNKS, *range(CHUNKS)):
            halo(1, piece).start()

    late = (depth == 0) & (core == 0)
    on(exists(-1) & jnp.logical_not(late), send_left)

    def row_slice(block, half):
        return rows_ref.at[pl.ds(block * CH + half * HALF, HALF)]

    def row_copy(kind, half, source, target_block, target):
        return remote(
            row_slice(source, half), row_slice(target_block, half),
            row_send.at[kind, half], row_recv.at[target_block - 1, half], target,
        )

    def to_sibling(half):
        return row_copy(0, half, 0, 1, me - 1)

    def to_two(half):
        return row_copy(1, half, 0, 2, me - 2)

    def to_four(half):
        return row_copy(2, half, 0, 4, me - 4)

    wide_row = lax.broadcasted_iota(jnp.int32, (HALF, 128), 0) + HALF
    wide_lane = lax.broadcasted_iota(jnp.int32, (HALF, 128), 1)
    band_row = lax.broadcasted_iota(jnp.int32, (CHUNK, CHUNK), 0) // BAND
    band_col = lax.broadcasted_iota(jnp.int32, (CHUNK, CHUNK), 1) // BAND

    def whiten(half):
        there = ((half == 1) & exists(1)) | ((half == 0) & exists(-1))
        low = pl.multiple_of(half * HALF, HALF)

        @pl.when(there)
        def _():
            for piece in (CHUNKS, *range(CHUNKS)):
                on(half == 0, halo(0, piece).wait_recv)
                on(half == 1, halo(1, piece).wait_recv)

        @pl.when(jnp.logical_not(there))
        def _():
            spec[pl.ds(pl.multiple_of(half * (CH + HALF), HALF), HALF), :] = jnp.zeros((HALF, 2 * FB), jnp.float32)
            labels[3 + half] = jnp.zeros((8, 128), jnp.int32)

        place = wide_row + low
        mine = jnp.where(wide_lane == place, labels[0, 0:1, :], 0).astype(jnp.float32)
        mine = jnp.sum(mine, axis=1, keepdims=True).astype(jnp.int32)
        wide = labels[0, 0:1, :] + labels[3 + half, 0:1, :]
        keep = (jnp.abs(wide_lane - place) <= HALF_WIN) & ((wide >> 1) == (mine >> 1)) & ((wide & 1) == 1)
        inside = jnp.where(keep, 1.0, 0.0)
        divisor = jnp.maximum(jnp.sum(inside, axis=1, keepdims=True), 1.0)
        alive = (mine & 1).astype(jnp.float32)
        weights = jnp.where(half == 1, pltpu.roll(inside, 128 - HALF, 1), inside)[:, : 3 * HALF].astype(jnp.bfloat16)
        weights = jnp.concatenate([weights, weights, weights], axis=1)
        same = jnp.where(band_row == band_col, 1.0, 0.0).astype(jnp.bfloat16)
        for c in range(CHUNKS):
            parts = []
            for offset in (c * WIDE, c * WIDE + CHUNK):
                cols = slice(offset, offset + CHUNK)
                stack = jnp.concatenate(split3(spec[pl.ds(low, 3 * HALF), cols]), axis=0)
                sums = dot(weights, stack)
                value = spec[pl.ds(pl.multiple_of(HALF + low, HALF), HALF), cols]
                parts.append(alive * (value * alive - sums / divisor))
            square = parts[0] * parts[0] + parts[1] * parts[1]
            sums = dot(jnp.concatenate(split3(square), axis=0), same)
            power = (sums[:HALF] + (sums[HALF : 2 * HALF] + sums[2 * HALF :])) * (1.0 / BAND)
            scale = lax.rsqrt(power + WHITEN_EPS)
            for part, offset in zip(parts, (c * WIDE, c * WIDE + CHUNK)):
                white = (part * scale).astype(jnp.bfloat16)
                rows_ref[pl.ds(low, HALF), offset : offset + CHUNK] = white
                own[pl.ds(low, HALF), offset : offset + CHUNK] = white.astype(jnp.float32)

    def blank(block):
        rows_ref[block * CH : (block + 1) * CH, :] = jnp.zeros((CH, 2 * FB), jnp.bfloat16)

    for block in range(1, REACH + 1):
        on(jnp.logical_not(exists(block)), functools.partial(blank, block))

    def arrived(block, half):
        row_copy(0, half, 0, block, me).wait_recv()

    def to_next(block, half):
        return row_copy(3 if block == 2 else 4, half, block, block - 1, me + 1)

    def forward(block):
        for half in (1, 0):
            on(exists(block), functools.partial(arrived, block, half))
            on(exists(block) & (core == 0), to_next(block, half).start)
            if block == 2:
                on(exists(block) & (core == 1), row_copy(3, half, block, 3, me - 1).start)

    def catch_up():
        def relay_late():
            meet(1)
            relay()

        on((depth == 0) & exists(-2), relay_late)
        on(exists(-4), lambda: meet(2))
        for half in (1, 0):
            @pl.when((half == 1) | jnp.logical_not(late))
            def _():
                on((depth == 0) & exists(-2), to_two(half).start)
                on(exists(-4), to_four(half).start)

    early = jnp.logical_not(late)

    def stage(t, carry):
        @pl.when((t == 0) | ((t == 1) & early) | ((t == 5) & late))
        def _():
            half = jnp.where((t == 1) | ((t == 0) & late), 1, 0)
            whiten(half)
            on(core == 1, to_sibling(half).start)
            on(((depth > 0) | (t == 5)) & exists(-2), to_two(half).start)
            on((depth > 1) & (t == 0) & exists(-4), lambda: meet(2))
            on(((depth > 1) | (t == 5)) & exists(-4), to_four(half).start)

        @pl.when((t == 2) | ((t == 3) & early) | (t == 4) | ((t >= 6) & late))
        def _():
            @pl.when(t == 2)
            def _():
                forward(2)
                for half in (1, 0):
                    on(exists(1), functools.partial(arrived, 1, half))
                load_table.wait()

            @pl.when(t == 4)
            def _():
                on(exists(-1) & late, send_left)
                on(depth <= 1, catch_up)
                forward(4)
                for half in (1, 0):
                    on(exists(3), functools.partial(arrived, 3, half))

            half = jnp.where((t == 2) | (t == 4), 1, 0)
            pair = jnp.where((t == 4) | (t == 7), 1, 0)
            near_rows = pl.ds(pl.multiple_of(half * HALF, HALF), HALF)
            far_rows = pl.ds(pl.multiple_of(CH + pair * 2 * CH, CH), 2 * CH)
            part_ref[near_rows, pl.ds(pl.multiple_of(pair * 2 * CH, CH), 2 * CH), :] = correlate(
                lambda cols: own[near_rows, cols], lambda cols: rows_ref[far_rows, cols], table, (HALF, 2 * CH, LAGS)
            )

        return carry

    lax.fori_loop(0, jnp.where(late, 8, 5), stage, 0)

    for side in (0, 1):
        for piece in range(CHUNKS + 1):
            on(exists(1 - 2 * side), halo(side, piece).wait_send)
    for half in (1, 0):
        on(core == 1, to_sibling(half).wait_send)
        on(exists(-2), to_two(half).wait_send)
        on(exists(-4), to_four(half).wait_send)
    for half in (1, 0):
        on(exists(2), to_next(2, half).wait_send)
        on(exists(4) & (core == 0), to_next(4, half).wait_send)


def finish_kernel(rows_ref, part_ref, table_ref, out_ref, done, sem):
    me = lax.axis_index("fiber")
    late = (lax.rem(me, 2) == 0) & (lax.rem(me // 2, 8) == 0)
    below, above = pl.ds(0, HALF), pl.ds(HALF, HALF)
    first, second = pl.ds(0, 2 * CH), pl.ds(2 * CH, 2 * CH)
    upper = pltpu.make_async_copy(part_ref.at[above], out_ref.at[above], sem.at[0])
    lower = pltpu.make_async_copy(part_ref.at[below, first], out_ref.at[below, first], sem.at[1])
    rest = pltpu.make_async_copy(done, out_ref.at[below, second], sem.at[2])
    rest_there = pltpu.make_async_copy(part_ref.at[below, second], out_ref.at[below, second], sem.at[2])
    upper.start()
    lower.start()
    pl.when(late)(rest_there.start)

    @pl.when(jnp.logical_not(late))
    def _():
        done[...] = correlate(
            lambda cols: rows_ref[below, cols].astype(jnp.float32),
            lambda cols: rows_ref[3 * CH :, cols],
            table_ref,
            (HALF, 2 * CH, LAGS),
        )
        rest.start()

    upper.wait()
    lower.wait()
    rest.wait()


def on_device(traces, live, segment):
    count = lax.axis_size("fiber")
    channels, length = traces.shape
    base, twiddle, lags = (jnp.asarray(t) for t in tables(length))
    in_hbm = pl.BlockSpec(memory_space=pltpu.HBM)
    in_vmem = pl.BlockSpec(memory_space=pltpu.VMEM)
    spans = -(-length // SPAN)
    rows, part = pl.pallas_call(
        functools.partial(spectra_kernel, count),
        out_shape=(
            jax.ShapeDtypeStruct(((1 + REACH) * channels, 2 * FB), jnp.bfloat16),
            jax.ShapeDtypeStruct((channels, REACH * channels, LAGS), jnp.bfloat16),
        ),
        in_specs=[in_hbm] * 6,
        out_specs=(in_vmem, in_vmem),
        scratch_shapes=[
            pltpu.VMEM((channels, length), jnp.float32),
            pltpu.VMEM((1, channels), jnp.int32),
            pltpu.VMEM((1, channels), jnp.int32),
            pltpu.VMEM((CHUNKS, 2, SPAN, WIDE), jnp.bfloat16),
            pltpu.VMEM((2, FB), jnp.float32),
            pltpu.VMEM((2 * FB, LAGS), jnp.bfloat16),
            pltpu.VMEM((spans * CH, SPAN), jnp.bfloat16),
            pltpu.VMEM((spans * CH, SPAN), jnp.bfloat16),
            pltpu.VMEM((2 * CH, 2 * FB), jnp.float32),
            pltpu.VMEM((5, 8, 128), jnp.int32),
            pltpu.VMEM((8, 128), jnp.int32),
            pltpu.VMEM((CH, 2 * FB), jnp.float32),
            pltpu.SemaphoreType.DMA((5 + CHUNKS,)),
            pltpu.SemaphoreType.REGULAR((3,)),
            pltpu.SemaphoreType.DMA((2, CHUNKS + 1)),
            pltpu.SemaphoreType.DMA((2, CHUNKS + 1)),
            pltpu.SemaphoreType.DMA((5, 2)),
            pltpu.SemaphoreType.DMA((4, 2)),
        ],
        compiler_params=pltpu.CompilerParams(
            collective_id=0, has_side_effects=True, vmem_limit_bytes=40 * 1024 * 1024
        ),
        name="spectra",
    )(
        *(
            pltpu.with_memory_space_constraint(x, pltpu.HBM)
            for x in (traces, live.reshape(1, channels), segment.reshape(1, channels), base, twiddle, lags)
        )
    )
    return pl.pallas_call(
        finish_kernel,
        out_shape=jax.ShapeDtypeStruct((channels, REACH * channels, LAGS), jnp.bfloat16),
        in_specs=[in_vmem] * 3,
        out_specs=in_hbm,
        scratch_shapes=[
            pltpu.VMEM((HALF, 2 * CH, LAGS), jnp.bfloat16),
            pltpu.SemaphoreType.DMA((3,)),
        ],
        compiler_params=pltpu.CompilerParams(vmem_limit_bytes=40 * 1024 * 1024),
        name="finish",
    )(rows, part, lags)


def solution(mesh):
    return jax.shard_map(
        on_device,
        mesh=mesh,
        in_specs=(P("fiber", None), P("fiber"), P("fiber")),
        out_specs=P("fiber", None, None),
        check_vma=False,
    )
```

```python
import functools
import math

import jax
import jax.numpy as jnp
import ml_dtypes
import numpy as np
from jax import lax
from jax.experimental import pallas as pl
from jax.experimental.pallas import tpu as pltpu
from jax.sharding import PartitionSpec as P

LOW_BIN = 32
FB = 768
BAND = 64
HALF_WIN = 15
LAGS = 256
CH = 32
HALF = 16
REACH = 4
SPAN = 256
CHUNK = 256
WHITEN_EPS = 1.0
MESH = pl.DeviceIdType.MESH


CHUNKS = FB // CHUNK
WIDE = 2 * CHUNK


def chunk_major(table, axis):
    halves = np.split(table, 2, axis=axis)
    pieces = [np.split(half, CHUNKS, axis=axis) for half in halves]
    return [np.concatenate([pieces[0][c], pieces[1][c]], axis=axis) for c in range(CHUNKS)]


def tables(length):
    bins = LOW_BIN + np.arange(FB)
    taper = np.sin(np.pi * (np.arange(FB) + 0.5) / FB)
    angle = 2.0 * np.pi / length * np.mod(np.arange(SPAN)[:, None] * bins[None, :], length)
    base = np.concatenate([np.cos(angle) * taper, -np.sin(angle) * taper], axis=1)
    base = np.stack(chunk_major(base, 1))
    high = base.astype(ml_dtypes.bfloat16)
    low = (base - high.astype(np.float64)).astype(ml_dtypes.bfloat16)
    turn = 2.0 * np.pi / length * np.mod(SPAN * bins, length)
    twiddle = np.stack([np.cos(turn), -np.sin(turn)]).astype(np.float32)
    lag = np.arange(LAGS) - LAGS // 2
    phase = 2.0 * np.pi / length * np.mod(bins[:, None] * lag[None, :], length)
    lags = np.concatenate([np.cos(phase), -np.sin(phase)], axis=0) / math.sqrt(FB)
    lags = np.concatenate(chunk_major(lags.astype(np.float32), 0), axis=0)
    return np.stack([high, low], axis=1), twiddle, lags.astype(ml_dtypes.bfloat16)


def split3(value):
    first = value.astype(jnp.bfloat16)
    rest = value - first.astype(jnp.float32)
    second = rest.astype(jnp.bfloat16)
    third = (rest - second.astype(jnp.float32)).astype(jnp.bfloat16)
    return first, second, third


def dot(a, b):
    return jnp.dot(a, b, preferred_element_type=jnp.float32)


def columns(start, width=CHUNK):
    return pl.ds(start if isinstance(start, int) else pl.multiple_of(start, CHUNK), width)


def correlate(own, far, table_ref, shape):
    total = None
    for c in range(CHUNKS):
        re_cols = slice(c * WIDE, c * WIDE + CHUNK)
        im_cols = slice(c * WIDE + CHUNK, (c + 1) * WIDE)
        own_re = own(re_cols)[:, None]
        own_im = own(im_cols)[:, None]
        far_re = far(re_cols).astype(jnp.float32)[None]
        far_im = far(im_cols).astype(jnp.float32)[None]
        flat = (own_re.shape[0] * far_re.shape[1], CHUNK)
        real = (own_re * far_re + own_im * far_im).astype(jnp.bfloat16).reshape(flat)
        imag = (own_im * far_re - own_re * far_im).astype(jnp.bfloat16).reshape(flat)
        term = dot(real, table_ref[re_cols, :]) + dot(imag, table_ref[im_cols, :])
        total = term if total is None else total + term
    return total.astype(jnp.bfloat16).reshape(shape)


def spectra_kernel(
    count,
    traces_hbm, live_hbm, segment_hbm, base_hbm, twiddle_hbm, table_hbm,
    rows_ref, part_ref,
    traces, live, segment, base, twiddle, table, first, second, spec, labels, whole, own,
    in_sem, here_sem, halo_send, halo_recv, row_send, row_recv,
):
    me = lax.axis_index("fiber")
    core = lax.rem(me, 2)
    depth = lax.rem(me // 2, 8)
    length = traces.shape[1]
    spans = -(-length // SPAN)

    barrier = pltpu.get_barrier_semaphore()

    def exists(step):
        return (me + step >= 0) & (me + step < count)

    def on(condition, action):
        pl.when(condition)(action)

    def signal(semaphore, step):
        pl.semaphore_signal(semaphore, inc=1, device_id=(me + step,), device_id_type=MESH)

    for step in (1, 2):
        on(exists(-step), functools.partial(signal, barrier, -step))
    on((depth < 7) & exists(2), functools.partial(signal, barrier, 2))

    small = [
        pltpu.make_async_copy(live_hbm, live, in_sem.at[0]),
        pltpu.make_async_copy(segment_hbm, segment, in_sem.at[1]),
        pltpu.make_async_copy(twiddle_hbm, twiddle, in_sem.at[2]),
    ]
    load_traces = pltpu.make_async_copy(traces_hbm, traces, in_sem.at[3])
    load_base = [pltpu.make_async_copy(base_hbm.at[c], base.at[c], in_sem.at[4 + c]) for c in range(CHUNKS)]
    load_table = pltpu.make_async_copy(table_hbm, table, in_sem.at[4 + CHUNKS])
    for load in (load_traces, *small, *load_base, load_table):
        load.start()

    def meet(slot):
        pl.semaphore_wait(here_sem.at[slot], 1)

    def greet():
        awaited = (exists(1), exists(2), (depth > 0) & exists(-2))
        peers = sum(jnp.where(peer, 1, 0) for peer in awaited)
        on(peers > 0, lambda: pl.semaphore_wait(barrier, peers))
        on(exists(1), functools.partial(signal, here_sem.at[0], 1))
        on((depth == 7) & exists(2), functools.partial(signal, here_sem.at[1], 2))

    last = depth == 7

    whole[...] = jnp.zeros_like(whole)
    for load in small:
        load.wait()
    whole[0:1, 0:CH] = segment[...] * 2 + live[...]
    packed = whole[...]
    lane = lax.broadcasted_iota(jnp.int32, (8, 128), 1)
    labels[0] = pltpu.roll(packed, HALF, 1)
    labels[1] = jnp.where(lane < HALF, pltpu.roll(packed, 128 - HALF, 1), 0)
    labels[2] = jnp.where((lane >= CH + HALF) & (lane < CH + 2 * HALF), pltpu.roll(packed, CH + HALF, 1), 0)

    def remote(src, dst, send, recv, target):
        return pltpu.make_async_remote_copy(
            src_ref=src, dst_ref=dst, send_sem=send, recv_sem=recv, device_id=(target,), device_id_type=MESH
        )

    def halo(side, piece):
        target = me + 1 if side == 0 else me - 1
        send, recv = halo_send.at[side, piece], halo_recv.at[side, piece]
        if isinstance(piece, int) and piece == CHUNKS:
            return remote(labels.at[1 + side], labels.at[3 + side], send, recv, target)
        cols = columns(piece * WIDE, WIDE)
        source, place = ((CH, 0), (HALF, CH + HALF))[side]
        return remote(spec.at[pl.ds(source, HALF), cols], spec.at[pl.ds(place, HALF), cols], send, recv, target)

    load_traces.wait()
    for s in range(spans):
        piece = traces[:, s * SPAN : min(length, (s + 1) * SPAN)]
        if piece.shape[1] < SPAN:
            piece = jnp.concatenate([piece, jnp.zeros((CH, SPAN - piece.shape[1]), jnp.float32)], axis=1)
        top = piece.astype(jnp.bfloat16)
        first[s * CH : (s + 1) * CH, :] = top
        second[s * CH : (s + 1) * CH, :] = (piece - top.astype(jnp.float32)).astype(jnp.bfloat16)

    def greet_first():
        greet()
        on(exists(1), halo(0, CHUNKS).start)

    on(last, greet_first)

    def transform(c, carry):
        pltpu.make_async_copy(base_hbm.at[c], base.at[c], in_sem.at[4 + c]).wait()
        parts = []
        for offset in (0, CHUNK):
            high, low = (base[c, k, :, offset : offset + CHUNK] for k in (0, 1))
            parts.append(dot(first[...], high) + dot(second[...], high) + dot(first[...], low))
        cosine = twiddle[0:1, columns(c * CHUNK)]
        sine = twiddle[1:2, columns(c * CHUNK)]
        real = parts[0][(spans - 1) * CH :, :]
        imag = parts[1][(spans - 1) * CH :, :]
        for s in range(spans - 2, -1, -1):
            rows = slice(s * CH, (s + 1) * CH)
            real, imag = (
                parts[0][rows, :] + (real * cosine - imag * sine),
                parts[1][rows, :] + (real * sine + imag * cosine),
            )
        spec[HALF : HALF + CH, columns(c * WIDE)] = real
        spec[HALF : HALF + CH, columns(c * WIDE + CHUNK)] = imag
        on(last & exists(1), halo(0, c).start)
        return carry

    lax.fori_loop(0, CHUNKS, transform, 0)

    def open_right():
        greet()
        for piece in (CHUNKS, *range(CHUNKS)):
            on(exists(1), halo(0, piece).start)

    on(jnp.logical_not(last), open_right)

    def send_left():
        meet(0)
        for piece in (CHUNKS, *range(CHUNKS)):
            halo(1, piece).start()

    late = (depth == 0) & (core == 0)
    on(exists(-1) & jnp.logical_not(late), send_left)

    def row_slice(block, half):
        return rows_ref.at[pl.ds(block * CH + half * HALF, HALF)]

    def row_copy(kind, half, source, target_block, target):
        return remote(
            row_slice(source, half), row_slice(target_block, half),
            row_send.at[kind, half], row_recv.at[target_block - 1, half], target,
        )

    def to_sibling(half):
        return row_copy(0, half, 0, 1, me - 1)

    def to_two(half):
        return row_copy(1, half, 0, 2, me - 2)

    def to_four(half):
        return row_copy(5, half, 0, 4, me - 4)

    def pass_on(half):
        return row_copy(2, half, 2, 4, me - 2)

    wide_row = lax.broadcasted_iota(jnp.int32, (HALF, 128), 0) + HALF
    wide_lane = lax.broadcasted_iota(jnp.int32, (HALF, 128), 1)
    band_row = lax.broadcasted_iota(jnp.int32, (CHUNK, CHUNK), 0) // BAND
    band_col = lax.broadcasted_iota(jnp.int32, (CHUNK, CHUNK), 1) // BAND

    def whiten(half):
        there = ((half == 1) & exists(1)) | ((half == 0) & exists(-1))
        low = pl.multiple_of(half * HALF, HALF)

        @pl.when(there)
        def _():
            for piece in (CHUNKS, *range(CHUNKS)):
                on(half == 0, halo(0, piece).wait_recv)
                on(half == 1, halo(1, piece).wait_recv)

        @pl.when(jnp.logical_not(there))
        def _():
            spec[pl.ds(pl.multiple_of(half * (CH + HALF), HALF), HALF), :] = jnp.zeros((HALF, 2 * FB), jnp.float32)
            labels[3 + half] = jnp.zeros((8, 128), jnp.int32)

        place = wide_row + low
        mine = jnp.where(wide_lane == place, labels[0, 0:1, :], 0).astype(jnp.float32)
        mine = jnp.sum(mine, axis=1, keepdims=True).astype(jnp.int32)
        wide = labels[0, 0:1, :] + labels[3 + half, 0:1, :]
        keep = (jnp.abs(wide_lane - place) <= HALF_WIN) & ((wide >> 1) == (mine >> 1)) & ((wide & 1) == 1)
        inside = jnp.where(keep, 1.0, 0.0)
        divisor = jnp.maximum(jnp.sum(inside, axis=1, keepdims=True), 1.0)
        alive = (mine & 1).astype(jnp.float32)
        weights = jnp.where(half == 1, pltpu.roll(inside, 128 - HALF, 1), inside)[:, : 3 * HALF].astype(jnp.bfloat16)
        weights = jnp.concatenate([weights, weights, weights], axis=1)
        same = jnp.where(band_row == band_col, 1.0, 0.0).astype(jnp.bfloat16)
        for c in range(CHUNKS):
            parts = []
            for offset in (c * WIDE, c * WIDE + CHUNK):
                cols = slice(offset, offset + CHUNK)
                stack = jnp.concatenate(split3(spec[pl.ds(low, 3 * HALF), cols]), axis=0)
                sums = dot(weights, stack)
                value = spec[pl.ds(pl.multiple_of(HALF + low, HALF), HALF), cols]
                parts.append(alive * (value * alive - sums / divisor))
            square = parts[0] * parts[0] + parts[1] * parts[1]
            sums = dot(jnp.concatenate(split3(square), axis=0), same)
            power = (sums[:HALF] + (sums[HALF : 2 * HALF] + sums[2 * HALF :])) * (1.0 / BAND)
            scale = lax.rsqrt(power + WHITEN_EPS)
            for part, offset in zip(parts, (c * WIDE, c * WIDE + CHUNK)):
                white = (part * scale).astype(jnp.bfloat16)
                rows_ref[pl.ds(low, HALF), offset : offset + CHUNK] = white
                own[pl.ds(low, HALF), offset : offset + CHUNK] = white.astype(jnp.float32)

    def blank(block):
        rows_ref[block * CH : (block + 1) * CH, :] = jnp.zeros((CH, 2 * FB), jnp.bfloat16)

    for block in range(1, REACH + 1):
        on(jnp.logical_not(exists(block)), functools.partial(blank, block))

    def arrived(block, half):
        row_copy(0, half, 0, block, me).wait_recv()

    def to_next(block, half):
        return row_copy(3 if block == 2 else 4, half, block, block - 1, me + 1)

    def forward(block):
        for half in (0, 1):
            on(exists(block), functools.partial(arrived, block, half))
            if block == 2:
                on(exists(block) & (depth > 0) & (depth < 7) & exists(-2), pass_on(half).start)
                on(exists(block) & (core == 1), row_copy(3, half, block, 3, me - 1).start)
            on(exists(block) & (core == 0), to_next(block, half).start)

    def catch_up():
        meet(1)
        for half in (1, 0):
            @pl.when((half == 1) | jnp.logical_not(late))
            def _():
                on(exists(-4), to_four(half).start)
                to_two(half).start()

        for half in (0, 1):
            on(exists(2), pass_on(half).start)

    early = jnp.logical_not(late)

    def stage(t, carry):
        @pl.when((t == 0) | ((t == 1) & early) | ((t == 5) & late))
        def _():
            half = jnp.where((t == 1) | ((t == 0) & late), 1, 0)
            whiten(half)
            on((t == 5) & exists(-4), to_four(half).start)
            on(((depth > 0) | (t == 5)) & exists(-2), to_two(half).start)
            on(core == 1, to_sibling(half).start)

        @pl.when((t == 2) | ((t == 3) & early) | (t == 4) | ((t >= 6) & late))
        def _():
            on(t == jnp.where(last & (core == 0), 4, 2), lambda: forward(2))

            @pl.when(t == jnp.where(last, 2, jnp.where((core == 0) & early, 3, 4)))
            def _():
                on(exists(-1) & late, send_left)
                on((depth == 0) & exists(-2), catch_up)
                forward(4)

            on(t == 2, load_table.wait)
            pair = jnp.where((t == 4) | (t == 7), 1, 0)
            pair = jnp.where(last, 1 - pair, pair)
            for block in (1, 3):
                for piece in (0, 1):
                    on(
                        ((t == 2) | (t == 4)) & (pair == block // 2) & exists(block),
                        functools.partial(arrived, block, piece),
                    )

            half = jnp.where((t == 2) | (t == 4), 1, 0)
            near_rows = pl.ds(pl.multiple_of(half * HALF, HALF), HALF)
            far_rows = pl.ds(pl.multiple_of(CH + pair * 2 * CH, CH), 2 * CH)
            part_ref[near_rows, pl.ds(pl.multiple_of(pair * 2 * CH, CH), 2 * CH), :] = correlate(
                lambda cols: own[near_rows, cols], lambda cols: rows_ref[far_rows, cols], table, (HALF, 2 * CH, LAGS)
            )

        return carry

    lax.fori_loop(0, jnp.where(late, 8, 5), stage, 0)

    for side in (0, 1):
        for piece in range(CHUNKS + 1):
            on(exists(1 - 2 * side), halo(side, piece).wait_send)
    for half in (1, 0):
        on(core == 1, to_sibling(half).wait_send)
        on(exists(-2), to_two(half).wait_send)
        on(exists(2) & (depth < 7) & exists(-2), pass_on(half).wait_send)
        on((depth == 0) & exists(-4), to_four(half).wait_send)
    for half in (1, 0):
        on(exists(2), to_next(2, half).wait_send)
        on(exists(4) & (core == 0), to_next(4, half).wait_send)


def finish_kernel(rows_ref, part_ref, table_ref, out_ref, done, sem):
    me = lax.axis_index("fiber")
    depth = lax.rem(me // 2, 8)
    late = (lax.rem(me, 2) == 0) & (depth == 0)
    start = pl.multiple_of(jnp.where(depth == 7, 0, 2 * CH), 2 * CH)
    below, above = pl.ds(0, HALF), pl.ds(HALF, HALF)
    first, second = pl.ds(pl.multiple_of(2 * CH - start, 2 * CH), 2 * CH), pl.ds(start, 2 * CH)
    far_rows = pl.ds(pl.multiple_of(CH + start, CH), 2 * CH)
    upper = pltpu.make_async_copy(part_ref.at[above], out_ref.at[above], sem.at[0])
    lower = pltpu.make_async_copy(part_ref.at[below, first], out_ref.at[below, first], sem.at[1])
    rest = pltpu.make_async_copy(done, out_ref.at[below, second], sem.at[2])
    rest_there = pltpu.make_async_copy(part_ref.at[below, second], out_ref.at[below, second], sem.at[2])
    upper.start()
    lower.start()
    pl.when(late)(rest_there.start)

    @pl.when(jnp.logical_not(late))
    def _():
        done[...] = correlate(
            lambda cols: rows_ref[below, cols].astype(jnp.float32),
            lambda cols: rows_ref[far_rows, cols],
            table_ref,
            (HALF, 2 * CH, LAGS),
        )
        rest.start()

    upper.wait()
    lower.wait()
    rest.wait()


def on_device(traces, live, segment):
    count = lax.axis_size("fiber")
    channels, length = traces.shape
    base, twiddle, lags = (jnp.asarray(t) for t in tables(length))
    in_hbm = pl.BlockSpec(memory_space=pltpu.HBM)
    in_vmem = pl.BlockSpec(memory_space=pltpu.VMEM)
    spans = -(-length // SPAN)
    rows, part = pl.pallas_call(
        functools.partial(spectra_kernel, count),
        out_shape=(
            jax.ShapeDtypeStruct(((1 + REACH) * channels, 2 * FB), jnp.bfloat16),
            jax.ShapeDtypeStruct((channels, REACH * channels, LAGS), jnp.bfloat16),
        ),
        in_specs=[in_hbm] * 6,
        out_specs=(in_vmem, in_vmem),
        scratch_shapes=[
            pltpu.VMEM((channels, length), jnp.float32),
            pltpu.VMEM((1, channels), jnp.int32),
            pltpu.VMEM((1, channels), jnp.int32),
            pltpu.VMEM((CHUNKS, 2, SPAN, WIDE), jnp.bfloat16),
            pltpu.VMEM((2, FB), jnp.float32),
            pltpu.VMEM((2 * FB, LAGS), jnp.bfloat16),
            pltpu.VMEM((spans * CH, SPAN), jnp.bfloat16),
            pltpu.VMEM((spans * CH, SPAN), jnp.bfloat16),
            pltpu.VMEM((2 * CH, 2 * FB), jnp.float32),
            pltpu.VMEM((5, 8, 128), jnp.int32),
            pltpu.VMEM((8, 128), jnp.int32),
            pltpu.VMEM((CH, 2 * FB), jnp.float32),
            pltpu.SemaphoreType.DMA((5 + CHUNKS,)),
            pltpu.SemaphoreType.REGULAR((2,)),
            pltpu.SemaphoreType.DMA((2, CHUNKS + 1)),
            pltpu.SemaphoreType.DMA((2, CHUNKS + 1)),
            pltpu.SemaphoreType.DMA((6, 2)),
            pltpu.SemaphoreType.DMA((4, 2)),
        ],
        compiler_params=pltpu.CompilerParams(
            collective_id=0, has_side_effects=True, vmem_limit_bytes=40 * 1024 * 1024
        ),
        name="spectra",
    )(
        *(
            pltpu.with_memory_space_constraint(x, pltpu.HBM)
            for x in (traces, live.reshape(1, channels), segment.reshape(1, channels), base, twiddle, lags)
        )
    )
    return pl.pallas_call(
        finish_kernel,
        out_shape=jax.ShapeDtypeStruct((channels, REACH * channels, LAGS), jnp.bfloat16),
        in_specs=[in_vmem] * 3,
        out_specs=in_hbm,
        scratch_shapes=[
            pltpu.VMEM((HALF, 2 * CH, LAGS), jnp.bfloat16),
            pltpu.SemaphoreType.DMA((3,)),
        ],
        compiler_params=pltpu.CompilerParams(vmem_limit_bytes=40 * 1024 * 1024),
        name="finish",
    )(rows, part, lags)


def solution(mesh):
    return jax.shard_map(
        on_device,
        mesh=mesh,
        in_specs=(P("fiber", None), P("fiber"), P("fiber")),
        out_specs=P("fiber", None, None),
        check_vma=False,
    )
```

```python
import functools
import math

import jax
import jax.numpy as jnp
import ml_dtypes
import numpy as np
from jax import lax
from jax.experimental import pallas as pl
from jax.experimental.pallas import tpu as pltpu
from jax.sharding import PartitionSpec as P

LOW_BIN = 32
FB = 768
BAND = 64
HALF_WIN = 15
LAGS = 256
CH = 32
HALF = 16
REACH = 4
SPAN = 256
CHUNK = 256
WHITEN_EPS = 1.0
MESH = pl.DeviceIdType.MESH


CHUNKS = FB // CHUNK
WIDE = 2 * CHUNK


def chunk_major(table, axis):
    halves = np.split(table, 2, axis=axis)
    pieces = [np.split(half, CHUNKS, axis=axis) for half in halves]
    return [np.concatenate([pieces[0][c], pieces[1][c]], axis=axis) for c in range(CHUNKS)]


def tables(length):
    bins = LOW_BIN + np.arange(FB)
    taper = np.sin(np.pi * (np.arange(FB) + 0.5) / FB)
    angle = 2.0 * np.pi / length * np.mod(np.arange(SPAN)[:, None] * bins[None, :], length)
    base = np.concatenate([np.cos(angle) * taper, -np.sin(angle) * taper], axis=1)
    base = np.stack(chunk_major(base, 1))
    high = base.astype(ml_dtypes.bfloat16)
    low = (base - high.astype(np.float64)).astype(ml_dtypes.bfloat16)
    turn = 2.0 * np.pi / length * np.mod(SPAN * bins, length)
    twiddle = np.stack([np.cos(turn), -np.sin(turn)]).astype(np.float32)
    lag = np.arange(LAGS) - LAGS // 2
    phase = 2.0 * np.pi / length * np.mod(bins[:, None] * lag[None, :], length)
    lags = np.concatenate([np.cos(phase), -np.sin(phase)], axis=0) / math.sqrt(FB)
    lags = np.concatenate(chunk_major(lags.astype(np.float32), 0), axis=0)
    return np.stack([high, low], axis=1), twiddle, lags.astype(ml_dtypes.bfloat16)


def split3(value):
    first = value.astype(jnp.bfloat16)
    rest = value - first.astype(jnp.float32)
    second = rest.astype(jnp.bfloat16)
    third = (rest - second.astype(jnp.float32)).astype(jnp.bfloat16)
    return first, second, third


def dot(a, b):
    return jnp.dot(a, b, preferred_element_type=jnp.float32)


def columns(start, width=CHUNK):
    return pl.ds(start if isinstance(start, int) else pl.multiple_of(start, CHUNK), width)


def correlate(own, far, table_ref, shape):
    total = None
    for c in range(CHUNKS):
        re_cols = slice(c * WIDE, c * WIDE + CHUNK)
        im_cols = slice(c * WIDE + CHUNK, (c + 1) * WIDE)
        own_re = own(re_cols)[:, None]
        own_im = own(im_cols)[:, None]
        far_re = far(re_cols).astype(jnp.float32)[None]
        far_im = far(im_cols).astype(jnp.float32)[None]
        flat = (own_re.shape[0] * far_re.shape[1], CHUNK)
        real = (own_re * far_re + own_im * far_im).astype(jnp.bfloat16).reshape(flat)
        imag = (own_im * far_re - own_re * far_im).astype(jnp.bfloat16).reshape(flat)
        term = dot(real, table_ref[re_cols, :]) + dot(imag, table_ref[im_cols, :])
        total = term if total is None else total + term
    return total.astype(jnp.bfloat16).reshape(shape)


def spectra_kernel(
    count,
    traces_hbm, live_hbm, segment_hbm, base_hbm, twiddle_hbm, table_hbm,
    rows_ref, part_ref,
    traces, live, segment, base, twiddle, table, first, second, spec, labels, whole, own,
    in_sem, here_sem, halo_send, halo_recv, row_send, row_recv,
):
    me = lax.axis_index("fiber")
    core = lax.rem(me, 2)
    depth = lax.rem(me // 2, 8)
    length = traces.shape[1]
    spans = -(-length // SPAN)

    barrier = pltpu.get_barrier_semaphore()

    def exists(step):
        return (me + step >= 0) & (me + step < count)

    def on(condition, action):
        pl.when(condition)(action)

    def signal(semaphore, step):
        pl.semaphore_signal(semaphore, inc=1, device_id=(me + step,), device_id_type=MESH)

    for step in (1, 2):
        on(exists(-step), functools.partial(signal, barrier, -step))
    on((depth < 6) & exists(2), functools.partial(signal, barrier, 2))

    small = [
        pltpu.make_async_copy(live_hbm, live, in_sem.at[0]),
        pltpu.make_async_copy(segment_hbm, segment, in_sem.at[1]),
        pltpu.make_async_copy(twiddle_hbm, twiddle, in_sem.at[2]),
    ]
    load_traces = pltpu.make_async_copy(traces_hbm, traces, in_sem.at[3])
    load_base = [pltpu.make_async_copy(base_hbm.at[c], base.at[c], in_sem.at[4 + c]) for c in range(CHUNKS)]
    load_table = pltpu.make_async_copy(table_hbm, table, in_sem.at[4 + CHUNKS])
    for load in (load_traces, *small, *load_base, load_table):
        load.start()

    def meet(slot):
        pl.semaphore_wait(here_sem.at[slot], 1)

    def greet():
        awaited = (exists(1), exists(2), (depth > 0) & (depth < 7) & exists(-2))
        peers = sum(jnp.where(peer, 1, 0) for peer in awaited)
        on(peers > 0, lambda: pl.semaphore_wait(barrier, peers))
        on(exists(1), functools.partial(signal, here_sem.at[0], 1))
        on((depth >= 6) & exists(2), functools.partial(signal, here_sem.at[1], 2))

    last = depth == 7
    on(last, greet)

    whole[...] = jnp.zeros_like(whole)
    for load in small:
        load.wait()
    whole[0:1, 0:CH] = segment[...] * 2 + live[...]
    packed = whole[...]
    lane = lax.broadcasted_iota(jnp.int32, (8, 128), 1)
    labels[0] = pltpu.roll(packed, HALF, 1)
    labels[1] = jnp.where(lane < HALF, pltpu.roll(packed, 128 - HALF, 1), 0)
    labels[2] = jnp.where((lane >= CH + HALF) & (lane < CH + 2 * HALF), pltpu.roll(packed, CH + HALF, 1), 0)

    def remote(src, dst, send, recv, target):
        return pltpu.make_async_remote_copy(
            src_ref=src, dst_ref=dst, send_sem=send, recv_sem=recv, device_id=(target,), device_id_type=MESH
        )

    def halo(side, piece):
        target = me + 1 if side == 0 else me - 1
        send, recv = halo_send.at[side, piece], halo_recv.at[side, piece]
        if isinstance(piece, int) and piece == CHUNKS:
            return remote(labels.at[1 + side], labels.at[3 + side], send, recv, target)
        cols = columns(piece * WIDE, WIDE)
        source, place = ((CH, 0), (HALF, CH + HALF))[side]
        return remote(spec.at[pl.ds(source, HALF), cols], spec.at[pl.ds(place, HALF), cols], send, recv, target)

    load_traces.wait()
    for s in range(spans):
        piece = traces[:, s * SPAN : min(length, (s + 1) * SPAN)]
        if piece.shape[1] < SPAN:
            piece = jnp.concatenate([piece, jnp.zeros((CH, SPAN - piece.shape[1]), jnp.float32)], axis=1)
        top = piece.astype(jnp.bfloat16)
        first[s * CH : (s + 1) * CH, :] = top
        second[s * CH : (s + 1) * CH, :] = (piece - top.astype(jnp.float32)).astype(jnp.bfloat16)

    on(last & exists(1), halo(0, CHUNKS).start)

    def transform(c, carry):
        pltpu.make_async_copy(base_hbm.at[c], base.at[c], in_sem.at[4 + c]).wait()
        parts = []
        for offset in (0, CHUNK):
            high, low = (base[c, k, :, offset : offset + CHUNK] for k in (0, 1))
            parts.append(dot(first[...], high) + dot(second[...], high) + dot(first[...], low))
        cosine = twiddle[0:1, columns(c * CHUNK)]
        sine = twiddle[1:2, columns(c * CHUNK)]
        real = parts[0][(spans - 1) * CH :, :]
        imag = parts[1][(spans - 1) * CH :, :]
        for s in range(spans - 2, -1, -1):
            rows = slice(s * CH, (s + 1) * CH)
            real, imag = (
                parts[0][rows, :] + (real * cosine - imag * sine),
                parts[1][rows, :] + (real * sine + imag * cosine),
            )
        spec[HALF : HALF + CH, columns(c * WIDE)] = real
        spec[HALF : HALF + CH, columns(c * WIDE + CHUNK)] = imag
        on(last & exists(1), halo(0, c).start)
        return carry

    lax.fori_loop(0, CHUNKS, transform, 0)

    def open_right():
        greet()
        for piece in (CHUNKS, *range(CHUNKS)):
            on(exists(1), halo(0, piece).start)

    on(jnp.logical_not(last), open_right)

    def relay():
        meet(1)
        on((core == 0) & exists(2), functools.partial(signal, here_sem.at[2], 2))

    on(last, relay)

    def send_left():
        meet(0)
        for piece in (CHUNKS, *range(CHUNKS)):
            halo(1, piece).start()

    late = (depth == 0) & (core == 0)
    on(exists(-1) & jnp.logical_not(late), send_left)

    def row_slice(block, half):
        return rows_ref.at[pl.ds(block * CH + half * HALF, HALF)]

    def row_copy(kind, half, source, target_block, target):
        return remote(
            row_slice(source, half), row_slice(target_block, half),
            row_send.at[kind, half], row_recv.at[target_block - 1, half], target,
        )

    def to_sibling(half):
        return row_copy(0, half, 0, 1, me - 1)

    def to_two(half):
        return row_copy(1, half, 0, 2, me - 2)

    def to_four(half):
        return row_copy(5, half, 0, 4, me - 4)

    def pass_on(half):
        return row_copy(2, half, 2, 4, me - 2)

    wide_row = lax.broadcasted_iota(jnp.int32, (HALF, 128), 0) + HALF
    wide_lane = lax.broadcasted_iota(jnp.int32, (HALF, 128), 1)
    band_row = lax.broadcasted_iota(jnp.int32, (CHUNK, CHUNK), 0) // BAND
    band_col = lax.broadcasted_iota(jnp.int32, (CHUNK, CHUNK), 1) // BAND

    def whiten(half):
        there = ((half == 1) & exists(1)) | ((half == 0) & exists(-1))
        low = pl.multiple_of(half * HALF, HALF)

        @pl.when(there)
        def _():
            for piece in (CHUNKS, *range(CHUNKS)):
                on(half == 0, halo(0, piece).wait_recv)
                on(half == 1, halo(1, piece).wait_recv)

        @pl.when(jnp.logical_not(there))
        def _():
            spec[pl.ds(pl.multiple_of(half * (CH + HALF), HALF), HALF), :] = jnp.zeros((HALF, 2 * FB), jnp.float32)
            labels[3 + half] = jnp.zeros((8, 128), jnp.int32)

        place = wide_row + low
        mine = jnp.where(wide_lane == place, labels[0, 0:1, :], 0).astype(jnp.float32)
        mine = jnp.sum(mine, axis=1, keepdims=True).astype(jnp.int32)
        wide = labels[0, 0:1, :] + labels[3 + half, 0:1, :]
        keep = (jnp.abs(wide_lane - place) <= HALF_WIN) & ((wide >> 1) == (mine >> 1)) & ((wide & 1) == 1)
        inside = jnp.where(keep, 1.0, 0.0)
        divisor = jnp.maximum(jnp.sum(inside, axis=1, keepdims=True), 1.0)
        alive = (mine & 1).astype(jnp.float32)
        weights = jnp.where(half == 1, pltpu.roll(inside, 128 - HALF, 1), inside)[:, : 3 * HALF].astype(jnp.bfloat16)
        weights = jnp.concatenate([weights, weights, weights], axis=1)
        same = jnp.where(band_row == band_col, 1.0, 0.0).astype(jnp.bfloat16)
        for c in range(CHUNKS):
            parts = []
            for offset in (c * WIDE, c * WIDE + CHUNK):
                cols = slice(offset, offset + CHUNK)
                stack = jnp.concatenate(split3(spec[pl.ds(low, 3 * HALF), cols]), axis=0)
                sums = dot(weights, stack)
                value = spec[pl.ds(pl.multiple_of(HALF + low, HALF), HALF), cols]
                parts.append(alive * (value * alive - sums / divisor))
            square = parts[0] * parts[0] + parts[1] * parts[1]
            sums = dot(jnp.concatenate(split3(square), axis=0), same)
            power = (sums[:HALF] + (sums[HALF : 2 * HALF] + sums[2 * HALF :])) * (1.0 / BAND)
            scale = lax.rsqrt(power + WHITEN_EPS)
            for part, offset in zip(parts, (c * WIDE, c * WIDE + CHUNK)):
                white = (part * scale).astype(jnp.bfloat16)
                rows_ref[pl.ds(low, HALF), offset : offset + CHUNK] = white
                own[pl.ds(low, HALF), offset : offset + CHUNK] = white.astype(jnp.float32)

    def blank(block):
        rows_ref[block * CH : (block + 1) * CH, :] = jnp.zeros((CH, 2 * FB), jnp.bfloat16)

    for block in range(1, REACH + 1):
        on(jnp.logical_not(exists(block)), functools.partial(blank, block))

    def arrived(block, half):
        row_copy(0, half, 0, block, me).wait_recv()

    def to_next(block, half):
        return row_copy(3 if block == 2 else 4, half, block, block - 1, me + 1)

    last_low = last & (core == 0)

    def passes(half):
        return exists(2) & exists(-2) & jnp.logical_not(last_low & (half == 0))

    def forward(block, half):
        on(exists(block), functools.partial(arrived, block, half))
        if block == 2:
            on(passes(half), pass_on(half).start)
            on(exists(block) & (core == 1), row_copy(3, half, block, 3, me - 1).start)
        on(exists(block) & (core == 0), to_next(block, half).start)

    def catch_up():
        meet(1)
        to_two(1).start()
        on(jnp.logical_not(late), to_two(0).start)

    early = jnp.logical_not(late)

    def stage(t, carry):
        @pl.when((t == 0) | ((t == 1) & early) | ((t == 5) & late))
        def _():
            half = jnp.where((t == 1) | ((t == 0) & late), 1, 0)
            whiten(half)
            on(((depth > 0) | (t == 5)) & exists(-2), to_two(half).start)
            on(core == 1, to_sibling(half).start)

            @pl.when((t == 5) & exists(-4))
            def _():
                meet(2)
                to_four(half).start()

        @pl.when((t == 2) | ((t == 3) & early) | (t == 4) | ((t >= 6) & late))
        def _():
            @pl.when(t == 2)
            def _():
                on(exists(-1) & late, send_left)
                on((depth == 0) & exists(-2), catch_up)
                on(jnp.logical_not(last_low), lambda: forward(2, 0))
                forward(2, 1)

            on((t == 4) & last_low, lambda: forward(2, 0))

            @pl.when(t == jnp.where(last, 2, jnp.where((core == 0) & early, 3, 4)))
            def _():
                forward(4, 0)
                forward(4, 1)

            on(t == 2, load_table.wait)
            pair = jnp.where((t == 4) | (t == 7), 1, 0)
            pair = jnp.where(last, 1 - pair, pair)
            for block in (1, 3):
                for piece in (0, 1):
                    on(
                        ((t == 2) | (t == 4)) & (pair == block // 2) & exists(block),
                        functools.partial(arrived, block, piece),
                    )

            half = jnp.where((t == 2) | (t == 4), 1, 0)
            near_rows = pl.ds(pl.multiple_of(half * HALF, HALF), HALF)
            far_rows = pl.ds(pl.multiple_of(CH + pair * 2 * CH, CH), 2 * CH)
            part_ref[near_rows, pl.ds(pl.multiple_of(pair * 2 * CH, CH), 2 * CH), :] = correlate(
                lambda cols: own[near_rows, cols], lambda cols: rows_ref[far_rows, cols], table, (HALF, 2 * CH, LAGS)
            )

        return carry

    lax.fori_loop(0, jnp.where(late, 8, 5), stage, 0)

    for side in (0, 1):
        for piece in range(CHUNKS + 1):
            on(exists(1 - 2 * side), halo(side, piece).wait_send)
    for half in (1, 0):
        on(core == 1, to_sibling(half).wait_send)
        on(exists(-2), to_two(half).wait_send)
        on(passes(half), pass_on(half).wait_send)
    on(late & exists(-4), to_four(0).wait_send)
    for half in (1, 0):
        on(exists(2), to_next(2, half).wait_send)
        on(exists(4) & (core == 0), to_next(4, half).wait_send)


def finish_kernel(rows_ref, part_ref, table_ref, out_ref, done, sem):
    me = lax.axis_index("fiber")
    depth = lax.rem(me // 2, 8)
    late = (lax.rem(me, 2) == 0) & (depth == 0)
    start = pl.multiple_of(jnp.where(depth == 7, 0, 2 * CH), 2 * CH)
    below, above = pl.ds(0, HALF), pl.ds(HALF, HALF)
    first, second = pl.ds(pl.multiple_of(2 * CH - start, 2 * CH), 2 * CH), pl.ds(start, 2 * CH)
    far_rows = pl.ds(pl.multiple_of(CH + start, CH), 2 * CH)
    upper = pltpu.make_async_copy(part_ref.at[above], out_ref.at[above], sem.at[0])
    lower = pltpu.make_async_copy(part_ref.at[below, first], out_ref.at[below, first], sem.at[1])
    rest = pltpu.make_async_copy(done, out_ref.at[below, second], sem.at[2])
    rest_there = pltpu.make_async_copy(part_ref.at[below, second], out_ref.at[below, second], sem.at[2])
    upper.start()
    lower.start()
    pl.when(late)(rest_there.start)

    @pl.when(jnp.logical_not(late))
    def _():
        done[...] = correlate(
            lambda cols: rows_ref[below, cols].astype(jnp.float32),
            lambda cols: rows_ref[far_rows, cols],
            table_ref,
            (HALF, 2 * CH, LAGS),
        )
        rest.start()

    upper.wait()
    lower.wait()
    rest.wait()


def on_device(traces, live, segment):
    count = lax.axis_size("fiber")
    channels, length = traces.shape
    base, twiddle, lags = (jnp.asarray(t) for t in tables(length))
    in_hbm = pl.BlockSpec(memory_space=pltpu.HBM)
    in_vmem = pl.BlockSpec(memory_space=pltpu.VMEM)
    spans = -(-length // SPAN)
    rows, part = pl.pallas_call(
        functools.partial(spectra_kernel, count),
        out_shape=(
            jax.ShapeDtypeStruct(((1 + REACH) * channels, 2 * FB), jnp.bfloat16),
            jax.ShapeDtypeStruct((channels, REACH * channels, LAGS), jnp.bfloat16),
        ),
        in_specs=[in_hbm] * 6,
        out_specs=(in_vmem, in_vmem),
        scratch_shapes=[
            pltpu.VMEM((channels, length), jnp.float32),
            pltpu.VMEM((1, channels), jnp.int32),
            pltpu.VMEM((1, channels), jnp.int32),
            pltpu.VMEM((CHUNKS, 2, SPAN, WIDE), jnp.bfloat16),
            pltpu.VMEM((2, FB), jnp.float32),
            pltpu.VMEM((2 * FB, LAGS), jnp.bfloat16),
            pltpu.VMEM((spans * CH, SPAN), jnp.bfloat16),
            pltpu.VMEM((spans * CH, SPAN), jnp.bfloat16),
            pltpu.VMEM((2 * CH, 2 * FB), jnp.float32),
            pltpu.VMEM((5, 8, 128), jnp.int32),
            pltpu.VMEM((8, 128), jnp.int32),
            pltpu.VMEM((CH, 2 * FB), jnp.float32),
            pltpu.SemaphoreType.DMA((5 + CHUNKS,)),
            pltpu.SemaphoreType.REGULAR((3,)),
            pltpu.SemaphoreType.DMA((2, CHUNKS + 1)),
            pltpu.SemaphoreType.DMA((2, CHUNKS + 1)),
            pltpu.SemaphoreType.DMA((6, 2)),
            pltpu.SemaphoreType.DMA((4, 2)),
        ],
        compiler_params=pltpu.CompilerParams(
            collective_id=0, has_side_effects=True, vmem_limit_bytes=40 * 1024 * 1024
        ),
        name="spectra",
    )(
        *(
            pltpu.with_memory_space_constraint(x, pltpu.HBM)
            for x in (traces, live.reshape(1, channels), segment.reshape(1, channels), base, twiddle, lags)
        )
    )
    return pl.pallas_call(
        finish_kernel,
        out_shape=jax.ShapeDtypeStruct((channels, REACH * channels, LAGS), jnp.bfloat16),
        in_specs=[in_vmem] * 3,
        out_specs=in_hbm,
        scratch_shapes=[
            pltpu.VMEM((HALF, 2 * CH, LAGS), jnp.bfloat16),
            pltpu.SemaphoreType.DMA((3,)),
        ],
        compiler_params=pltpu.CompilerParams(vmem_limit_bytes=40 * 1024 * 1024),
        name="finish",
    )(rows, part, lags)


def solution(mesh):
    return jax.shard_map(
        on_device,
        mesh=mesh,
        in_specs=(P("fiber", None), P("fiber"), P("fiber")),
        out_specs=P("fiber", None, None),
        check_vma=False,
    )
```

```python
import functools
import math

import jax
import jax.numpy as jnp
import ml_dtypes
import numpy as np
from jax import lax
from jax.experimental import pallas as pl
from jax.experimental.pallas import tpu as pltpu
from jax.sharding import PartitionSpec as P

LOW_BIN = 32
FB = 768
BAND = 64
HALF_WIN = 15
LAGS = 256
CH = 32
HALF = 16
REACH = 4
SPAN = 256
CHUNK = 256
WHITEN_EPS = 1.0
MESH = pl.DeviceIdType.MESH


CHUNKS = FB // CHUNK
WIDE = 2 * CHUNK


def chunk_major(table, axis):
    halves = np.split(table, 2, axis=axis)
    pieces = [np.split(half, CHUNKS, axis=axis) for half in halves]
    return [np.concatenate([pieces[0][c], pieces[1][c]], axis=axis) for c in range(CHUNKS)]


def tables(length):
    bins = LOW_BIN + np.arange(FB)
    taper = np.sin(np.pi * (np.arange(FB) + 0.5) / FB)
    angle = 2.0 * np.pi / length * np.mod(np.arange(SPAN)[:, None] * bins[None, :], length)
    base = np.concatenate([np.cos(angle) * taper, -np.sin(angle) * taper], axis=1)
    base = np.stack(chunk_major(base, 1))
    high = base.astype(ml_dtypes.bfloat16)
    low = (base - high.astype(np.float64)).astype(ml_dtypes.bfloat16)
    turn = 2.0 * np.pi / length * np.mod(SPAN * bins, length)
    twiddle = np.stack([np.cos(turn), -np.sin(turn)]).astype(np.float32)
    lag = np.arange(LAGS) - LAGS // 2
    phase = 2.0 * np.pi / length * np.mod(bins[:, None] * lag[None, :], length)
    lags = np.concatenate([np.cos(phase), -np.sin(phase)], axis=0) / math.sqrt(FB)
    lags = np.concatenate(chunk_major(lags.astype(np.float32), 0), axis=0)
    return np.stack([high, low], axis=1), twiddle, lags.astype(ml_dtypes.bfloat16)


def split3(value):
    first = value.astype(jnp.bfloat16)
    rest = value - first.astype(jnp.float32)
    second = rest.astype(jnp.bfloat16)
    third = (rest - second.astype(jnp.float32)).astype(jnp.bfloat16)
    return first, second, third


def dot(a, b):
    return jnp.dot(a, b, preferred_element_type=jnp.float32)


def columns(start, width=CHUNK):
    return pl.ds(start if isinstance(start, int) else pl.multiple_of(start, CHUNK), width)


def correlate(own, far, table_ref, shape):
    total = None
    for c in range(CHUNKS):
        re_cols = slice(c * WIDE, c * WIDE + CHUNK)
        im_cols = slice(c * WIDE + CHUNK, (c + 1) * WIDE)
        own_re = own(re_cols)[:, None]
        own_im = own(im_cols)[:, None]
        far_re = far(re_cols).astype(jnp.float32)[None]
        far_im = far(im_cols).astype(jnp.float32)[None]
        flat = (own_re.shape[0] * far_re.shape[1], CHUNK)
        real = (own_re * far_re + own_im * far_im).astype(jnp.bfloat16).reshape(flat)
        imag = (own_im * far_re - own_re * far_im).astype(jnp.bfloat16).reshape(flat)
        term = dot(real, table_ref[re_cols, :]) + dot(imag, table_ref[im_cols, :])
        total = term if total is None else total + term
    return total.astype(jnp.bfloat16).reshape(shape)


def spectra_kernel(
    count,
    traces_hbm, live_hbm, segment_hbm, base_hbm, twiddle_hbm, table_hbm,
    rows_ref, part_ref,
    traces, live, segment, base, twiddle, table, first, second, spec, labels, whole, own,
    in_sem, here_sem, halo_send, halo_recv, row_send, row_recv,
):
    me = lax.axis_index("fiber")
    core = lax.rem(me, 2)
    depth = lax.rem(me // 2, 8)
    length = traces.shape[1]
    spans = -(-length // SPAN)

    barrier = pltpu.get_barrier_semaphore()

    def exists(step):
        return (me + step >= 0) & (me + step < count)

    def on(condition, action):
        pl.when(condition)(action)

    def signal(semaphore, step):
        pl.semaphore_signal(semaphore, inc=1, device_id=(me + step,), device_id_type=MESH)

    for step in (1, 2):
        on(exists(-step), functools.partial(signal, barrier, -step))
    on((depth < 6) & exists(2), functools.partial(signal, barrier, 2))

    small = [
        pltpu.make_async_copy(live_hbm, live, in_sem.at[0]),
        pltpu.make_async_copy(segment_hbm, segment, in_sem.at[1]),
        pltpu.make_async_copy(twiddle_hbm, twiddle, in_sem.at[2]),
    ]
    load_traces = pltpu.make_async_copy(traces_hbm, traces, in_sem.at[3])
    load_base = [pltpu.make_async_copy(base_hbm.at[c], base.at[c], in_sem.at[4 + c]) for c in range(CHUNKS)]
    load_table = pltpu.make_async_copy(table_hbm, table, in_sem.at[4 + CHUNKS])
    for load in (load_traces, *small, *load_base, load_table):
        load.start()

    def meet(slot):
        pl.semaphore_wait(here_sem.at[slot], 1)

    def greet():
        awaited = (exists(1), exists(2), (depth > 0) & (depth < 7) & exists(-2))
        peers = sum(jnp.where(peer, 1, 0) for peer in awaited)
        on(peers > 0, lambda: pl.semaphore_wait(barrier, peers))
        on(exists(1), functools.partial(signal, here_sem.at[0], 1))
        on((depth >= 6) & exists(2), functools.partial(signal, here_sem.at[1], 2))

    last = depth == 7
    on(last, greet)

    whole[...] = jnp.zeros_like(whole)
    for load in small:
        load.wait()
    whole[0:1, 0:CH] = segment[...] * 2 + live[...]
    packed = whole[...]
    lane = lax.broadcasted_iota(jnp.int32, (8, 128), 1)
    labels[0] = pltpu.roll(packed, HALF, 1)
    labels[1] = jnp.where(lane < HALF, pltpu.roll(packed, 128 - HALF, 1), 0)
    labels[2] = jnp.where((lane >= CH + HALF) & (lane < CH + 2 * HALF), pltpu.roll(packed, CH + HALF, 1), 0)

    def remote(src, dst, send, recv, target):
        return pltpu.make_async_remote_copy(
            src_ref=src, dst_ref=dst, send_sem=send, recv_sem=recv, device_id=(target,), device_id_type=MESH
        )

    def halo(side, piece):
        target = me + 1 if side == 0 else me - 1
        send, recv = halo_send.at[side, piece], halo_recv.at[side, piece]
        if isinstance(piece, int) and piece == CHUNKS:
            return remote(labels.at[1 + side], labels.at[3 + side], send, recv, target)
        cols = columns(piece * WIDE, WIDE)
        source, place = ((CH, 0), (HALF, CH + HALF))[side]
        return remote(spec.at[pl.ds(source, HALF), cols], spec.at[pl.ds(place, HALF), cols], send, recv, target)

    load_traces.wait()
    for s in range(spans):
        piece = traces[:, s * SPAN : min(length, (s + 1) * SPAN)]
        if piece.shape[1] < SPAN:
            piece = jnp.concatenate([piece, jnp.zeros((CH, SPAN - piece.shape[1]), jnp.float32)], axis=1)
        top = piece.astype(jnp.bfloat16)
        first[s * CH : (s + 1) * CH, :] = top
        second[s * CH : (s + 1) * CH, :] = (piece - top.astype(jnp.float32)).astype(jnp.bfloat16)

    on(last & exists(1), halo(0, CHUNKS).start)

    def transform(c, carry):
        pltpu.make_async_copy(base_hbm.at[c], base.at[c], in_sem.at[4 + c]).wait()
        parts = []
        for offset in (0, CHUNK):
            high, low = (base[c, k, :, offset : offset + CHUNK] for k in (0, 1))
            parts.append(dot(first[...], high) + dot(second[...], high) + dot(first[...], low))
        cosine = twiddle[0:1, columns(c * CHUNK)]
        sine = twiddle[1:2, columns(c * CHUNK)]
        real = parts[0][(spans - 1) * CH :, :]
        imag = parts[1][(spans - 1) * CH :, :]
        for s in range(spans - 2, -1, -1):
            rows = slice(s * CH, (s + 1) * CH)
            real, imag = (
                parts[0][rows, :] + (real * cosine - imag * sine),
                parts[1][rows, :] + (real * sine + imag * cosine),
            )
        spec[HALF : HALF + CH, columns(c * WIDE)] = real
        spec[HALF : HALF + CH, columns(c * WIDE + CHUNK)] = imag
        on(last & exists(1), halo(0, c).start)
        return carry

    lax.fori_loop(0, CHUNKS, transform, 0)

    def open_right():
        greet()
        for piece in (CHUNKS, *range(CHUNKS)):
            on(exists(1), halo(0, piece).start)

    on(jnp.logical_not(last), open_right)

    def relay():
        meet(1)
        on((core == 0) & exists(2), functools.partial(signal, here_sem.at[2], 2))

    on(last, relay)

    def send_left():
        meet(0)
        for piece in (CHUNKS, *range(CHUNKS)):
            halo(1, piece).start()

    late = (depth == 0) & (core == 0)
    on(exists(-1) & jnp.logical_not(late), send_left)

    def row_slice(block, half):
        return rows_ref.at[pl.ds(block * CH + half * HALF, HALF)]

    def row_copy(kind, half, source, target_block, target):
        return remote(
            row_slice(source, half), row_slice(target_block, half),
            row_send.at[kind, half], row_recv.at[target_block - 1, half], target,
        )

    def to_sibling(half):
        return row_copy(0, half, 0, 1, me - 1)

    def to_two(half):
        return row_copy(1, half, 0, 2, me - 2)

    def to_four(half):
        return row_copy(5, half, 0, 4, me - 4)

    def pass_on(half):
        return row_copy(2, half, 2, 4, me - 2)

    wide_row = lax.broadcasted_iota(jnp.int32, (HALF, 128), 0) + HALF
    wide_lane = lax.broadcasted_iota(jnp.int32, (HALF, 128), 1)
    band_row = lax.broadcasted_iota(jnp.int32, (CHUNK, CHUNK), 0) // BAND
    band_col = lax.broadcasted_iota(jnp.int32, (CHUNK, CHUNK), 1) // BAND

    def whiten(half):
        there = ((half == 1) & exists(1)) | ((half == 0) & exists(-1))
        low = pl.multiple_of(half * HALF, HALF)

        @pl.when(there)
        def _():
            for piece in (CHUNKS, *range(CHUNKS)):
                on(half == 0, halo(0, piece).wait_recv)
                on(half == 1, halo(1, piece).wait_recv)

        @pl.when(jnp.logical_not(there))
        def _():
            spec[pl.ds(pl.multiple_of(half * (CH + HALF), HALF), HALF), :] = jnp.zeros((HALF, 2 * FB), jnp.float32)
            labels[3 + half] = jnp.zeros((8, 128), jnp.int32)

        place = wide_row + low
        mine = jnp.where(wide_lane == place, labels[0, 0:1, :], 0).astype(jnp.float32)
        mine = jnp.sum(mine, axis=1, keepdims=True).astype(jnp.int32)
        wide = labels[0, 0:1, :] + labels[3 + half, 0:1, :]
        keep = (jnp.abs(wide_lane - place) <= HALF_WIN) & ((wide >> 1) == (mine >> 1)) & ((wide & 1) == 1)
        inside = jnp.where(keep, 1.0, 0.0)
        divisor = jnp.maximum(jnp.sum(inside, axis=1, keepdims=True), 1.0)
        alive = (mine & 1).astype(jnp.float32)
        weights = jnp.where(half == 1, pltpu.roll(inside, 128 - HALF, 1), inside)[:, : 3 * HALF].astype(jnp.bfloat16)
        weights = jnp.concatenate([weights, weights, weights], axis=1)
        same = jnp.where(band_row == band_col, 1.0, 0.0).astype(jnp.bfloat16)
        for c in range(CHUNKS):
            parts = []
            for offset in (c * WIDE, c * WIDE + CHUNK):
                cols = slice(offset, offset + CHUNK)
                stack = jnp.concatenate(split3(spec[pl.ds(low, 3 * HALF), cols]), axis=0)
                sums = dot(weights, stack)
                value = spec[pl.ds(pl.multiple_of(HALF + low, HALF), HALF), cols]
                parts.append(alive * (value * alive - sums / divisor))
            square = parts[0] * parts[0] + parts[1] * parts[1]
            sums = dot(jnp.concatenate(split3(square), axis=0), same)
            power = (sums[:HALF] + (sums[HALF : 2 * HALF] + sums[2 * HALF :])) * (1.0 / BAND)
            scale = lax.rsqrt(power + WHITEN_EPS)
            for part, offset in zip(parts, (c * WIDE, c * WIDE + CHUNK)):
                white = (part * scale).astype(jnp.bfloat16)
                rows_ref[pl.ds(low, HALF), offset : offset + CHUNK] = white
                own[pl.ds(low, HALF), offset : offset + CHUNK] = white.astype(jnp.float32)

    def blank(block):
        rows_ref[block * CH : (block + 1) * CH, :] = jnp.zeros((CH, 2 * FB), jnp.bfloat16)

    for block in range(1, REACH + 1):
        on(jnp.logical_not(exists(block)), functools.partial(blank, block))

    def arrived(block, half):
        row_copy(0, half, 0, block, me).wait_recv()

    def to_next(block, half):
        return row_copy(3 if block == 2 else 4, half, block, block - 1, me + 1)

    last_low = last & (core == 0)

    def passes(half):
        return exists(2) & exists(-2) & jnp.logical_not(last_low & (half == 0))

    def forward(block, half):
        on(exists(block), functools.partial(arrived, block, half))
        if block == 2:
            on(passes(half), pass_on(half).start)
            on(exists(block) & (core == 1), row_copy(3, half, block, 3, me - 1).start)
        on(exists(block) & (core == 0), to_next(block, half).start)

    def hand_over():
        forward(4, 0)
        forward(4, 1)

    def take(block):
        for half in (0, 1):
            on(exists(block), functools.partial(arrived, block, half))

    def catch_up():
        meet(1)
        to_two(1).start()
        on(jnp.logical_not(late), to_two(0).start)

    early = jnp.logical_not(late)

    def stage(t, carry):
        @pl.when((t == 0) | ((t == 1) & early) | ((t == 5) & late))
        def _():
            half = jnp.where((t == 1) | ((t == 0) & late), 1, 0)
            whiten(half)
            on(((depth > 0) | (t == 5)) & exists(-2), to_two(half).start)
            on(core == 1, to_sibling(half).start)

            @pl.when((t == 5) & exists(-4))
            def _():
                meet(2)
                to_four(half).start()

        @pl.when((t >= 2) & early)
        def _():
            on((t == 2) & (depth == 0) & exists(-2), catch_up)
            on((t == 2) & last_low, lambda: forward(2, 1))
            turn = t - 2
            low_order = jnp.where(last & (turn > 0), jnp.where(turn == 3, 2, turn + 2), turn + 1)
            high_order = jnp.where(turn == 0, 2, jnp.where(turn == 1, 1, jnp.where(turn == 2, 4, 3)))
            high_last = jnp.where(turn == 0, 2, jnp.where(turn == 1, 4, jnp.where(turn == 2, 3, 1)))
            block = jnp.where(core == 0, low_order, jnp.where(last, high_last, high_order))
            for one in (1, 3):
                on(block == one, functools.partial(take, one))
            on(block == 2, lambda: forward(2, 0))
            on((block == 2) & jnp.logical_not(last_low), lambda: forward(2, 1))
            on(block == 4, hand_over)
            on(t == 2, load_table.wait)

            @pl.when(t < 5)
            def _():
                far_rows = pl.ds(pl.multiple_of(block * CH, CH), CH)
                part_ref[:, pl.ds(pl.multiple_of((block - 1) * CH, CH), CH), :] = correlate(
                    lambda cols: own[:, cols], lambda cols: rows_ref[far_rows, cols], table, (CH, CH, LAGS)
                )

        @pl.when(((t == 2) | (t == 4) | (t >= 6)) & late)
        def _():
            @pl.when(t == 2)
            def _():
                on(exists(-1), send_left)
                on(exists(-2), catch_up)
                forward(2, 0)
                forward(2, 1)
                take(1)
                load_table.wait()

            @pl.when(t == 4)
            def _():
                hand_over()
                take(3)

            half = jnp.where(t <= 4, 1, 0)
            pair = jnp.where((t == 4) | (t == 7), 1, 0)
            near_rows = pl.ds(pl.multiple_of(half * HALF, HALF), HALF)
            far_rows = pl.ds(pl.multiple_of(CH + pair * 2 * CH, CH), 2 * CH)
            part_ref[near_rows, pl.ds(pl.multiple_of(pair * 2 * CH, CH), 2 * CH), :] = correlate(
                lambda cols: own[near_rows, cols], lambda cols: rows_ref[far_rows, cols], table, (HALF, 2 * CH, LAGS)
            )

        return carry

    lax.fori_loop(0, jnp.where(late, 8, 6), stage, 0)

    for side in (0, 1):
        for piece in range(CHUNKS + 1):
            on(exists(1 - 2 * side), halo(side, piece).wait_send)
    for half in (1, 0):
        on(core == 1, to_sibling(half).wait_send)
        on(exists(-2), to_two(half).wait_send)
        on(passes(half), pass_on(half).wait_send)
    on(late & exists(-4), to_four(0).wait_send)
    for half in (1, 0):
        on(exists(2), to_next(2, half).wait_send)
        on(exists(4) & (core == 0), to_next(4, half).wait_send)


def finish_kernel(rows_ref, part_ref, table_ref, out_ref, done, sem):
    me = lax.axis_index("fiber")
    core, depth = lax.rem(me, 2), lax.rem(me // 2, 8)
    late = (core == 0) & (depth == 0)
    block = jnp.where(depth == 7, 1, 3) - core

    def place(step):
        return pl.ds(pl.multiple_of(lax.rem(block + step, REACH) * CH, CH), CH)

    def there(step):
        return pltpu.make_async_copy(part_ref.at[:, place(step)], out_ref.at[:, place(step)], sem.at[step])

    for step in range(1, REACH):
        there(step).start()
    pl.when(late)(there(0).start)
    rest = pltpu.make_async_copy(done, out_ref.at[:, place(0)], sem.at[0])

    @pl.when(jnp.logical_not(late))
    def _():
        far_rows = pl.ds(pl.multiple_of((block + 1) * CH, CH), CH)
        done[...] = correlate(
            lambda cols: rows_ref[0:CH, cols].astype(jnp.float32),
            lambda cols: rows_ref[far_rows, cols],
            table_ref,
            (CH, CH, LAGS),
        )
        rest.start()

    for step in range(1, REACH):
        there(step).wait()
    rest.wait()


def on_device(traces, live, segment):
    count = lax.axis_size("fiber")
    channels, length = traces.shape
    base, twiddle, lags = (jnp.asarray(t) for t in tables(length))
    in_hbm = pl.BlockSpec(memory_space=pltpu.HBM)
    in_vmem = pl.BlockSpec(memory_space=pltpu.VMEM)
    spans = -(-length // SPAN)
    rows, part = pl.pallas_call(
        functools.partial(spectra_kernel, count),
        out_shape=(
            jax.ShapeDtypeStruct(((1 + REACH) * channels, 2 * FB), jnp.bfloat16),
            jax.ShapeDtypeStruct((channels, REACH * channels, LAGS), jnp.bfloat16),
        ),
        in_specs=[in_hbm] * 6,
        out_specs=(in_vmem, in_vmem),
        scratch_shapes=[
            pltpu.VMEM((channels, length), jnp.float32),
            pltpu.VMEM((1, channels), jnp.int32),
            pltpu.VMEM((1, channels), jnp.int32),
            pltpu.VMEM((CHUNKS, 2, SPAN, WIDE), jnp.bfloat16),
            pltpu.VMEM((2, FB), jnp.float32),
            pltpu.VMEM((2 * FB, LAGS), jnp.bfloat16),
            pltpu.VMEM((spans * CH, SPAN), jnp.bfloat16),
            pltpu.VMEM((spans * CH, SPAN), jnp.bfloat16),
            pltpu.VMEM((2 * CH, 2 * FB), jnp.float32),
            pltpu.VMEM((5, 8, 128), jnp.int32),
            pltpu.VMEM((8, 128), jnp.int32),
            pltpu.VMEM((CH, 2 * FB), jnp.float32),
            pltpu.SemaphoreType.DMA((5 + CHUNKS,)),
            pltpu.SemaphoreType.REGULAR((3,)),
            pltpu.SemaphoreType.DMA((2, CHUNKS + 1)),
            pltpu.SemaphoreType.DMA((2, CHUNKS + 1)),
            pltpu.SemaphoreType.DMA((6, 2)),
            pltpu.SemaphoreType.DMA((4, 2)),
        ],
        compiler_params=pltpu.CompilerParams(
            collective_id=0, has_side_effects=True, vmem_limit_bytes=40 * 1024 * 1024
        ),
        name="spectra",
    )(
        *(
            pltpu.with_memory_space_constraint(x, pltpu.HBM)
            for x in (traces, live.reshape(1, channels), segment.reshape(1, channels), base, twiddle, lags)
        )
    )
    return pl.pallas_call(
        finish_kernel,
        out_shape=jax.ShapeDtypeStruct((channels, REACH * channels, LAGS), jnp.bfloat16),
        in_specs=[in_vmem] * 3,
        out_specs=in_hbm,
        scratch_shapes=[
            pltpu.VMEM((CH, CH, LAGS), jnp.bfloat16),
            pltpu.SemaphoreType.DMA((REACH,)),
        ],
        compiler_params=pltpu.CompilerParams(vmem_limit_bytes=40 * 1024 * 1024),
        name="finish",
    )(rows, part, lags)


def solution(mesh):
    return jax.shard_map(
        on_device,
        mesh=mesh,
        in_specs=(P("fiber", None), P("fiber"), P("fiber")),
        out_specs=P("fiber", None, None),
        check_vma=False,
    )
```

```python
import functools
import math

import jax
import jax.numpy as jnp
import ml_dtypes
import numpy as np
from jax import lax
from jax.experimental import pallas as pl
from jax.experimental.pallas import tpu as pltpu
from jax.sharding import PartitionSpec as P

LOW_BIN = 32
FB = 768
BAND = 64
HALF_WIN = 15
LAGS = 256
CH = 32
HALF = 16
REACH = 4
SPAN = 256
CHUNK = 256
WHITEN_EPS = 1.0
MESH = pl.DeviceIdType.MESH


CHUNKS = FB // CHUNK
WIDE = 2 * CHUNK


def chunk_major(table, axis):
    halves = np.split(table, 2, axis=axis)
    pieces = [np.split(half, CHUNKS, axis=axis) for half in halves]
    return [np.concatenate([pieces[0][c], pieces[1][c]], axis=axis) for c in range(CHUNKS)]


def tables(length):
    bins = LOW_BIN + np.arange(FB)
    taper = np.sin(np.pi * (np.arange(FB) + 0.5) / FB)
    angle = 2.0 * np.pi / length * np.mod(np.arange(SPAN)[:, None] * bins[None, :], length)
    base = np.concatenate([np.cos(angle) * taper, -np.sin(angle) * taper], axis=1)
    base = np.stack(chunk_major(base, 1))
    high = base.astype(ml_dtypes.bfloat16)
    low = (base - high.astype(np.float64)).astype(ml_dtypes.bfloat16)
    turn = 2.0 * np.pi / length * np.mod(SPAN * bins, length)
    twiddle = np.stack([np.cos(turn), -np.sin(turn)]).astype(np.float32)
    lag = np.arange(LAGS) - LAGS // 2
    phase = 2.0 * np.pi / length * np.mod(bins[:, None] * lag[None, :], length)
    lags = np.concatenate([np.cos(phase), -np.sin(phase)], axis=0) / math.sqrt(FB)
    lags = np.concatenate(chunk_major(lags.astype(np.float32), 0), axis=0)
    return np.stack([high, low], axis=1), twiddle, lags.astype(ml_dtypes.bfloat16)


def split3(value):
    first = value.astype(jnp.bfloat16)
    rest = value - first.astype(jnp.float32)
    second = rest.astype(jnp.bfloat16)
    third = (rest - second.astype(jnp.float32)).astype(jnp.bfloat16)
    return first, second, third


def dot(a, b):
    return jnp.dot(a, b, preferred_element_type=jnp.float32)


def columns(start, width=CHUNK):
    return pl.ds(start if isinstance(start, int) else pl.multiple_of(start, CHUNK), width)


def correlate(own, far, table_ref, shape):
    total = None
    for c in range(CHUNKS):
        re_cols = slice(c * WIDE, c * WIDE + CHUNK)
        im_cols = slice(c * WIDE + CHUNK, (c + 1) * WIDE)
        own_re = own(re_cols)[:, None]
        own_im = own(im_cols)[:, None]
        far_re = far(re_cols).astype(jnp.float32)[None]
        far_im = far(im_cols).astype(jnp.float32)[None]
        flat = (own_re.shape[0] * far_re.shape[1], CHUNK)
        real = (own_re * far_re + own_im * far_im).astype(jnp.bfloat16).reshape(flat)
        imag = (own_im * far_re - own_re * far_im).astype(jnp.bfloat16).reshape(flat)
        term = dot(real, table_ref[re_cols, :]) + dot(imag, table_ref[im_cols, :])
        total = term if total is None else total + term
    return total.astype(jnp.bfloat16).reshape(shape)


def spectra_kernel(
    count,
    traces_hbm, live_hbm, segment_hbm, base_hbm, twiddle_hbm, table_hbm,
    rows_ref, part_ref,
    traces, live, segment, base, twiddle, table, first, second, spec, labels, whole, own,
    in_sem, here_sem, halo_send, halo_recv, row_send, row_recv,
):
    me = lax.axis_index("fiber")
    core = lax.rem(me, 2)
    depth = lax.rem(me // 2, 8)
    length = traces.shape[1]
    spans = -(-length // SPAN)

    barrier = pltpu.get_barrier_semaphore()

    def exists(step):
        return (me + step >= 0) & (me + step < count)

    def on(condition, action):
        pl.when(condition)(action)

    def signal(semaphore, step):
        pl.semaphore_signal(semaphore, inc=1, device_id=(me + step,), device_id_type=MESH)

    for step in (1, 2):
        on(exists(-step), functools.partial(signal, barrier, -step))
    on((depth < 6) & exists(2), functools.partial(signal, barrier, 2))

    small = [
        pltpu.make_async_copy(live_hbm, live, in_sem.at[0]),
        pltpu.make_async_copy(segment_hbm, segment, in_sem.at[1]),
        pltpu.make_async_copy(twiddle_hbm, twiddle, in_sem.at[2]),
    ]
    load_traces = pltpu.make_async_copy(traces_hbm, traces, in_sem.at[3])
    load_base = [pltpu.make_async_copy(base_hbm.at[c], base.at[c], in_sem.at[4 + c]) for c in range(CHUNKS)]
    load_table = pltpu.make_async_copy(table_hbm, table, in_sem.at[4 + CHUNKS])
    for load in (load_traces, *small, *load_base, load_table):
        load.start()

    def meet(slot):
        pl.semaphore_wait(here_sem.at[slot], 1)

    def greet():
        awaited = (exists(1), exists(2), (depth > 0) & (depth < 7) & exists(-2))
        peers = sum(jnp.where(peer, 1, 0) for peer in awaited)
        on(peers > 0, lambda: pl.semaphore_wait(barrier, peers))
        on(exists(1), functools.partial(signal, here_sem.at[0], 1))
        on((depth >= 6) & exists(2), functools.partial(signal, here_sem.at[1], 2))

    last = depth == 7
    on(last, greet)

    whole[...] = jnp.zeros_like(whole)
    for load in small:
        load.wait()
    whole[0:1, 0:CH] = segment[...] * 2 + live[...]
    packed = whole[...]
    lane = lax.broadcasted_iota(jnp.int32, (8, 128), 1)
    labels[0] = pltpu.roll(packed, HALF, 1)
    labels[1] = jnp.where(lane < HALF, pltpu.roll(packed, 128 - HALF, 1), 0)
    labels[2] = jnp.where((lane >= CH + HALF) & (lane < CH + 2 * HALF), pltpu.roll(packed, CH + HALF, 1), 0)

    def remote(src, dst, send, recv, target):
        return pltpu.make_async_remote_copy(
            src_ref=src, dst_ref=dst, send_sem=send, recv_sem=recv, device_id=(target,), device_id_type=MESH
        )

    def halo(side, piece):
        target = me + 1 if side == 0 else me - 1
        send, recv = halo_send.at[side, piece], halo_recv.at[side, piece]
        if isinstance(piece, int) and piece == CHUNKS:
            return remote(labels.at[1 + side], labels.at[3 + side], send, recv, target)
        cols = columns(piece * WIDE, WIDE)
        source, place = ((CH, 0), (HALF, CH + HALF))[side]
        return remote(spec.at[pl.ds(source, HALF), cols], spec.at[pl.ds(place, HALF), cols], send, recv, target)

    load_traces.wait()
    for s in range(spans):
        piece = traces[:, s * SPAN : min(length, (s + 1) * SPAN)]
        if piece.shape[1] < SPAN:
            piece = jnp.concatenate([piece, jnp.zeros((CH, SPAN - piece.shape[1]), jnp.float32)], axis=1)
        top = piece.astype(jnp.bfloat16)
        first[s * CH : (s + 1) * CH, :] = top
        second[s * CH : (s + 1) * CH, :] = (piece - top.astype(jnp.float32)).astype(jnp.bfloat16)

    on(last & exists(1), halo(0, CHUNKS).start)

    def transform(c, carry):
        pltpu.make_async_copy(base_hbm.at[c], base.at[c], in_sem.at[4 + c]).wait()
        parts = []
        for offset in (0, CHUNK):
            high, low = (base[c, k, :, offset : offset + CHUNK] for k in (0, 1))
            parts.append(dot(first[...], high) + dot(second[...], high) + dot(first[...], low))
        cosine = twiddle[0:1, columns(c * CHUNK)]
        sine = twiddle[1:2, columns(c * CHUNK)]
        real = parts[0][(spans - 1) * CH :, :]
        imag = parts[1][(spans - 1) * CH :, :]
        for s in range(spans - 2, -1, -1):
            rows = slice(s * CH, (s + 1) * CH)
            real, imag = (
                parts[0][rows, :] + (real * cosine - imag * sine),
                parts[1][rows, :] + (real * sine + imag * cosine),
            )
        spec[HALF : HALF + CH, columns(c * WIDE)] = real
        spec[HALF : HALF + CH, columns(c * WIDE + CHUNK)] = imag
        on(last & exists(1), halo(0, c).start)
        return carry

    lax.fori_loop(0, CHUNKS, transform, 0)

    def open_right():
        greet()
        for piece in (CHUNKS, *range(CHUNKS)):
            on(exists(1), halo(0, piece).start)

    on(jnp.logical_not(last), open_right)

    def relay():
        meet(1)
        on((core == 0) & exists(2), functools.partial(signal, here_sem.at[2], 2))

    on(last, relay)

    def send_left():
        meet(0)
        for piece in (CHUNKS, *range(CHUNKS)):
            halo(1, piece).start()

    late = (depth == 0) & (core == 0)
    on(exists(-1) & jnp.logical_not(late), send_left)

    def row_slice(block, half):
        return rows_ref.at[pl.ds(block * CH + half * HALF, HALF)]

    def row_copy(kind, half, source, target_block, target):
        return remote(
            row_slice(source, half), row_slice(target_block, half),
            row_send.at[kind, half], row_recv.at[target_block - 1, half], target,
        )

    def to_sibling(half):
        return row_copy(0, half, 0, 1, me - 1)

    def to_two(half):
        return row_copy(1, half, 0, 2, me - 2)

    def to_four(half):
        return row_copy(5, half, 0, 4, me - 4)

    def pass_on(half):
        return row_copy(2, half, 2, 4, me - 2)

    wide_row = lax.broadcasted_iota(jnp.int32, (HALF, 128), 0) + HALF
    wide_lane = lax.broadcasted_iota(jnp.int32, (HALF, 128), 1)
    band_row = lax.broadcasted_iota(jnp.int32, (CHUNK, CHUNK), 0) // BAND
    band_col = lax.broadcasted_iota(jnp.int32, (CHUNK, CHUNK), 1) // BAND

    def whiten(half):
        there = ((half == 1) & exists(1)) | ((half == 0) & exists(-1))
        low = pl.multiple_of(half * HALF, HALF)

        @pl.when(there)
        def _():
            on(half == 0, halo(0, CHUNKS).wait_recv)
            on(half == 1, halo(1, CHUNKS).wait_recv)

        @pl.when(jnp.logical_not(there))
        def _():
            spec[pl.ds(pl.multiple_of(half * (CH + HALF), HALF), HALF), :] = jnp.zeros((HALF, 2 * FB), jnp.float32)
            labels[3 + half] = jnp.zeros((8, 128), jnp.int32)

        place = wide_row + low
        mine = jnp.where(wide_lane == place, labels[0, 0:1, :], 0).astype(jnp.float32)
        mine = jnp.sum(mine, axis=1, keepdims=True).astype(jnp.int32)
        wide = labels[0, 0:1, :] + labels[3 + half, 0:1, :]
        keep = (jnp.abs(wide_lane - place) <= HALF_WIN) & ((wide >> 1) == (mine >> 1)) & ((wide & 1) == 1)
        inside = jnp.where(keep, 1.0, 0.0)
        divisor = jnp.maximum(jnp.sum(inside, axis=1, keepdims=True), 1.0)
        alive = (mine & 1).astype(jnp.float32)
        weights = jnp.where(half == 1, pltpu.roll(inside, 128 - HALF, 1), inside)[:, : 3 * HALF].astype(jnp.bfloat16)
        weights = jnp.concatenate([weights, weights, weights], axis=1)
        share = alive / divisor

        @pl.when(there)
        def _():
            for piece in range(CHUNKS):
                on(half == 0, halo(0, piece).wait_recv)
                on(half == 1, halo(1, piece).wait_recv)

        same = jnp.where(band_row == band_col, 1.0, 0.0).astype(jnp.bfloat16)
        for c in range(CHUNKS):
            parts = []
            for offset in (c * WIDE, c * WIDE + CHUNK):
                cols = slice(offset, offset + CHUNK)
                stack = jnp.concatenate(split3(spec[pl.ds(low, 3 * HALF), cols]), axis=0)
                sums = dot(weights, stack)
                value = spec[pl.ds(pl.multiple_of(HALF + low, HALF), HALF), cols]
                parts.append(value * alive - sums * share)
            square = parts[0] * parts[0] + parts[1] * parts[1]
            sums = dot(jnp.concatenate(split3(square)[:2], axis=0), same)
            power = (sums[:HALF] + sums[HALF:]) * (1.0 / BAND)
            scale = lax.rsqrt(power + WHITEN_EPS)
            for part, offset in zip(parts, (c * WIDE, c * WIDE + CHUNK)):
                white = (part * scale).astype(jnp.bfloat16)
                rows_ref[pl.ds(low, HALF), offset : offset + CHUNK] = white
                own[pl.ds(low, HALF), offset : offset + CHUNK] = white.astype(jnp.float32)

    def blank(block):
        rows_ref[block * CH : (block + 1) * CH, :] = jnp.zeros((CH, 2 * FB), jnp.bfloat16)

    for block in range(1, REACH + 1):
        on(jnp.logical_not(exists(block)), functools.partial(blank, block))

    def arrived(block, half):
        row_copy(0, half, 0, block, me).wait_recv()

    def to_next(block, half):
        return row_copy(3 if block == 2 else 4, half, block, block - 1, me + 1)

    last_low = last & (core == 0)

    def passes(half):
        return exists(2) & exists(-2) & jnp.logical_not(last_low & (half == 0))

    def forward(block, half):
        on(exists(block), functools.partial(arrived, block, half))
        if block == 2:
            on(passes(half), pass_on(half).start)
            on(exists(block) & (core == 1), row_copy(3, half, block, 3, me - 1).start)
        on(exists(block) & (core == 0), to_next(block, half).start)

    def hand_over():
        forward(4, 0)
        forward(4, 1)

    def take(block):
        for half in (0, 1):
            on(exists(block), functools.partial(arrived, block, half))

    def catch_up():
        meet(1)
        to_two(1).start()
        on(jnp.logical_not(late), to_two(0).start)

    early = jnp.logical_not(late)

    def stage(t, carry):
        @pl.when((t == 0) | ((t == 1) & early) | ((t == 5) & late))
        def _():
            half = jnp.where((t == 1) | ((t == 0) & late), 1, 0)
            whiten(half)
            on(((depth > 0) | (t == 5)) & exists(-2), to_two(half).start)
            on(core == 1, to_sibling(half).start)

            @pl.when((t == 5) & exists(-4))
            def _():
                meet(2)
                to_four(half).start()

        @pl.when((t >= 2) & early)
        def _():
            on((t == 2) & (depth == 0) & exists(-2), catch_up)
            on((t == 2) & last_low, lambda: forward(2, 1))
            turn = t - 2
            low_order = jnp.where(last & (turn > 0), jnp.where(turn == 3, 2, turn + 2), turn + 1)
            high_order = jnp.where(turn == 0, 2, jnp.where(turn == 1, 1, jnp.where(turn == 2, 4, 3)))
            high_last = jnp.where(turn == 0, 2, jnp.where(turn == 1, 4, jnp.where(turn == 2, 3, 1)))
            block = jnp.where(core == 0, low_order, jnp.where(last, high_last, high_order))
            for one in (1, 3):
                on(block == one, functools.partial(take, one))
            on(block == 2, lambda: forward(2, 0))
            on((block == 2) & jnp.logical_not(last_low), lambda: forward(2, 1))
            on(block == 4, hand_over)
            on(t == 2, load_table.wait)

            @pl.when(t < 5)
            def _():
                far_rows = pl.ds(pl.multiple_of(block * CH, CH), CH)
                part_ref[:, pl.ds(pl.multiple_of((block - 1) * CH, CH), CH), :] = correlate(
                    lambda cols: own[:, cols], lambda cols: rows_ref[far_rows, cols], table, (CH, CH, LAGS)
                )

        @pl.when(((t == 2) | (t == 4) | (t >= 6)) & late)
        def _():
            @pl.when(t == 2)
            def _():
                on(exists(-1), send_left)
                on(exists(-2), catch_up)
                forward(2, 0)
                forward(2, 1)
                take(1)
                load_table.wait()

            @pl.when(t == 4)
            def _():
                hand_over()
                take(3)

            half = jnp.where(t <= 4, 1, 0)
            pair = jnp.where((t == 4) | (t == 7), 1, 0)
            near_rows = pl.ds(pl.multiple_of(half * HALF, HALF), HALF)
            far_rows = pl.ds(pl.multiple_of(CH + pair * 2 * CH, CH), 2 * CH)
            part_ref[near_rows, pl.ds(pl.multiple_of(pair * 2 * CH, CH), 2 * CH), :] = correlate(
                lambda cols: own[near_rows, cols], lambda cols: rows_ref[far_rows, cols], table, (HALF, 2 * CH, LAGS)
            )

        return carry

    lax.fori_loop(0, jnp.where(late, 8, 6), stage, 0)

    for side in (0, 1):
        for piece in range(CHUNKS + 1):
            on(exists(1 - 2 * side), halo(side, piece).wait_send)
    for half in (1, 0):
        on(core == 1, to_sibling(half).wait_send)
        on(exists(-2), to_two(half).wait_send)
        on(passes(half), pass_on(half).wait_send)
    on(late & exists(-4), to_four(0).wait_send)
    for half in (1, 0):
        on(exists(2), to_next(2, half).wait_send)
        on(exists(4) & (core == 0), to_next(4, half).wait_send)


def finish_kernel(rows_ref, part_ref, table_ref, out_ref, done, sem):
    me = lax.axis_index("fiber")
    core, depth = lax.rem(me, 2), lax.rem(me // 2, 8)
    late = (core == 0) & (depth == 0)
    block = jnp.where(depth == 7, 1, 3) - core

    def place(step):
        return pl.ds(pl.multiple_of(lax.rem(block + step, REACH) * CH, CH), CH)

    def there(step):
        return pltpu.make_async_copy(part_ref.at[:, place(step)], out_ref.at[:, place(step)], sem.at[step])

    for step in range(1, REACH):
        there(step).start()
    pl.when(late)(there(0).start)
    rest = pltpu.make_async_copy(done, out_ref.at[:, place(0)], sem.at[0])

    @pl.when(jnp.logical_not(late))
    def _():
        far_rows = pl.ds(pl.multiple_of((block + 1) * CH, CH), CH)
        done[...] = correlate(
            lambda cols: rows_ref[0:CH, cols].astype(jnp.float32),
            lambda cols: rows_ref[far_rows, cols],
            table_ref,
            (CH, CH, LAGS),
        )
        rest.start()

    for step in range(1, REACH):
        there(step).wait()
    rest.wait()


def on_device(traces, live, segment):
    count = lax.axis_size("fiber")
    channels, length = traces.shape
    base, twiddle, lags = (jnp.asarray(t) for t in tables(length))
    in_hbm = pl.BlockSpec(memory_space=pltpu.HBM)
    in_vmem = pl.BlockSpec(memory_space=pltpu.VMEM)
    spans = -(-length // SPAN)
    rows, part = pl.pallas_call(
        functools.partial(spectra_kernel, count),
        out_shape=(
            jax.ShapeDtypeStruct(((1 + REACH) * channels, 2 * FB), jnp.bfloat16),
            jax.ShapeDtypeStruct((channels, REACH * channels, LAGS), jnp.bfloat16),
        ),
        in_specs=[in_hbm] * 6,
        out_specs=(in_vmem, in_vmem),
        scratch_shapes=[
            pltpu.VMEM((channels, length), jnp.float32),
            pltpu.VMEM((1, channels), jnp.int32),
            pltpu.VMEM((1, channels), jnp.int32),
            pltpu.VMEM((CHUNKS, 2, SPAN, WIDE), jnp.bfloat16),
            pltpu.VMEM((2, FB), jnp.float32),
            pltpu.VMEM((2 * FB, LAGS), jnp.bfloat16),
            pltpu.VMEM((spans * CH, SPAN), jnp.bfloat16),
            pltpu.VMEM((spans * CH, SPAN), jnp.bfloat16),
            pltpu.VMEM((2 * CH, 2 * FB), jnp.float32),
            pltpu.VMEM((5, 8, 128), jnp.int32),
            pltpu.VMEM((8, 128), jnp.int32),
            pltpu.VMEM((CH, 2 * FB), jnp.float32),
            pltpu.SemaphoreType.DMA((5 + CHUNKS,)),
            pltpu.SemaphoreType.REGULAR((3,)),
            pltpu.SemaphoreType.DMA((2, CHUNKS + 1)),
            pltpu.SemaphoreType.DMA((2, CHUNKS + 1)),
            pltpu.SemaphoreType.DMA((6, 2)),
            pltpu.SemaphoreType.DMA((4, 2)),
        ],
        compiler_params=pltpu.CompilerParams(
            collective_id=0, has_side_effects=True, vmem_limit_bytes=40 * 1024 * 1024
        ),
        name="spectra",
    )(
        *(
            pltpu.with_memory_space_constraint(x, pltpu.HBM)
            for x in (traces, live.reshape(1, channels), segment.reshape(1, channels), base, twiddle, lags)
        )
    )
    return pl.pallas_call(
        finish_kernel,
        out_shape=jax.ShapeDtypeStruct((channels, REACH * channels, LAGS), jnp.bfloat16),
        in_specs=[in_vmem] * 3,
        out_specs=in_hbm,
        scratch_shapes=[
            pltpu.VMEM((CH, CH, LAGS), jnp.bfloat16),
            pltpu.SemaphoreType.DMA((REACH,)),
        ],
        compiler_params=pltpu.CompilerParams(vmem_limit_bytes=40 * 1024 * 1024),
        name="finish",
    )(rows, part, lags)


def solution(mesh):
    return jax.shard_map(
        on_device,
        mesh=mesh,
        in_specs=(P("fiber", None), P("fiber"), P("fiber")),
        out_specs=P("fiber", None, None),
        check_vma=False,
    )
```
